128 devices in a mesh: leaf: 16 (over z, y), help: 8 (over x, core).
Axes of the slice: x: 4, y: 4, z: 4, core: 2. Of those that a mesh axis runs over, the one named last changes fastest.
Arguments:
- points: float32 [64, 131072], P(None, ('leaf', 'help')), may hold values from -3 to 3
- weights: float32 [256, 131072], P(None, ('leaf', 'help')), may hold values from -0.12 to 0.12
- interp: float32 [256, 512, 256], P(('leaf', 'help')), may hold values from -0.25 to 0.25
- transfer: float32 [14, 512, 256], replicated, may hold values from -0.25 to 0.25
- near_count: int32 [16, 16], P('leaf', 'help'), may hold values from 1 to 32, 256 in all within a row
- near_src: int32 [256, 32], P(('leaf', 'help')), may hold values from 0 to 255, as said below
- skel_group: int32 [16, 256], P('leaf'), may hold values from 0 to 8191, as said below
- skel_node: int32 [14, 256], replicated, may hold values from 0 to 511, as said below
- far_nodes: int32 [30, 4], replicated, may hold values from 0 to 15, as said below
Outputs:
- product: float32 [256, 131072], P(None, ('leaf', 'help'))
The draws below stay inside these ranges and needn't reach their ends.
Inputs may be any that keep to these rules, and one draw needn't show every extreme that they name: `near_src`: slot 0 of leaf i names leaf i itself; every source of a leaf of subtree g is a leaf of subtree g - 1, g or g + 1. Slots at or after the leaf's near_count are not used. `near_count`: the 16 counts of one subtree sum to exactly 256. `skel_group`: each row holds 256 distinct indices into its subtree's points, counted from the subtree's first point. `skel_node`: each row holds 256 distinct indices into its two children's skeleton points, the first child's first. `far_nodes`: rows 0 to 15 are the level-0 nodes, the next 8 rows the level-1 nodes, and so on down to the 2 nodes of the highest listed level; each entry is a node number of that row's level. On level 0, the first entry of node k's row is k - 1 (modulo 16) and no other entry is k, k + 1 or k - 1 (modulo 16); on a higher level of c >= 4 nodes, no entry of node k's row is k, k + 1 or k - 1 (modulo c); on the level of 2 nodes, every entry is the other node.
All inputs are finite; a program needn't handle non-finite values. No bound on the sum of `near_count` on one device may be relied on, other than what follows from the above.
Results may differ from the reference program's by a relative error of at most 0.0003.
Values sent between devices are 32-bit elements; how exact they have to be, the bound alone decides.
A program may use at most 192 MiB of HBM per device.

```python
import math
import jax
import jax.numpy as jnp
import numpy as np
from jax import lax

F = 64
R = 256
LEAF = 512
SK = 256
NEAR = 32
NEAR_MEAN = 16
FL = 4
GROUPS = 16
LG = 16
NLEAF = 256
NPTS = 131072
NODES_UP = 14


def first_rows(key, rows, width, total):
    keys = jax.random.split(key, rows)
    return jax.vmap(lambda k: jax.random.permutation(k, total)[:width])(keys).astype(jnp.int32)


def draw_near_src(key, part):
    key = jax.random.fold_in(key, 11)
    leaf_ids = jnp.arange(NLEAF, dtype=jnp.int32)
    group = leaf_ids // LG
    step_key, pick_key = jax.random.split(key)
    offset = jax.random.randint(step_key, (NLEAF, NEAR), -1, 2).astype(jnp.int32)
    target = group[:, None] + offset
    target = jnp.where((target < 0) | (target >= GROUPS), group[:, None], target)
    within = jax.random.randint(pick_key, (NLEAF, NEAR), 0, LG).astype(jnp.int32)
    sources = target * LG + within
    sources = sources.at[:, 0].set(leaf_ids)
    return sources.astype(jnp.int32)


def draw_skel_group(key, part):
    key = jax.random.fold_in(key, 23)
    return first_rows(key, GROUPS, SK, LG * LEAF)


def draw_skel_node(key, part):
    key = jax.random.fold_in(key, 37)
    return first_rows(key, NODES_UP, SK, 2 * SK)


def draw_far_nodes(key, part):
    key = jax.random.fold_in(key, 41)
    pieces = []
    for level in range(GROUPS.bit_length() - 1):
        count = GROUPS >> level
        level_key = jax.random.fold_in(key, level)
        nodes = jnp.arange(count, dtype=jnp.int32)
        if count >= 4:
            if level == 0:
                first = ((nodes + count - 1) % count)[:, None]
            else:
                first = ((nodes + count // 2) % count)[:, None]
            steps = jax.random.randint(level_key, (count, FL - 1), 2, count - 1).astype(jnp.int32)
            others = (nodes[:, None] + steps) % count
            pieces.append(jnp.concatenate([first, others], axis=1))
        else:
            other = (nodes + 1) % count
            pieces.append(jnp.broadcast_to(other[:, None], (count, FL)))
    return jnp.concatenate(pieces, axis=0).astype(jnp.int32)


def level_of(rng, shape, cuts, smallest, top_value):
    factor_of = 1.0
    for axis_at, shards_of in cuts:
        draws = jax.random.uniform(jax.random.fold_in(jax.random.fold_in(rng, 6), axis_at), (shards_of,), jnp.float32, smallest / len(cuts), top_value / len(cuts))
        factor_of = factor_of * jnp.repeat(jnp.exp(draws), shape[axis_at] // shards_of).reshape((-1,) + (1,) * (len(shape) - 1 - axis_at))
    return factor_of


def profile(number_of, total, reach, slope):
    portions = [(1 << 20) // math.isqrt(standing ** slope) + 1 for standing in range(2, number_of + 1)]
    rest, given = total - reach - (number_of - 1), [1] * (number_of - 1)
    while rest > 0:
        candidates = [i for i in range(number_of - 1) if given[i] < reach]
        pool, remaining = sum([portions[i] for i in candidates]), rest
        for i in candidates:
            more = min(reach - given[i], max(1, remaining * portions[i] // pool), rest)
            given[i] = given[i] + more
            rest = rest - more
    return np.array([reach] + given)


def ragged_sizes(own_key, count, total, reach, lean):
    if count == 2:
        one = jax.random.randint(own_key, (), max(1, total - reach), min(reach, total - 1) + 1)
        return jnp.stack([one, total - one])
    sizes = jnp.asarray(profile(count, total, reach, lean), jnp.int32)
    couples = (count - 1) // 2
    source_of, sink = sizes[1:1 + 2 * couples:2], sizes[2:2 + 2 * couples:2]
    room = jnp.minimum(source_of - 1, reach - sink)
    shifted = jax.random.randint(jax.random.fold_in(own_key, 1), (couples,), 0, 1 << 20) % (room + 1)
    sizes = sizes.at[1:1 + 2 * couples:2].set(source_of - shifted).at[2:2 + 2 * couples:2].set(sink + shifted)
    return sizes[jax.random.permutation(jax.random.fold_in(own_key, 2), count)]


def normal_values(stream_key, extent, deviation, reach, cuts=(), held_as=jnp.bfloat16):
    values = jax.random.normal(stream_key, extent, jnp.float32) * deviation
    if len(cuts) > 0:
        values = level_of(stream_key, extent, cuts, -0.22, 0.18) * values
    return jnp.clip(values, min=-reach, max=reach).astype(held_as)


def setup_inputs(seed: int = 0) -> dict:
    streams_of = jax.random.split(jax.random.key(seed), 10)
    return {
        "points": normal_values(streams_of[0], (F, NPTS), 0.5, 3.0, ((1, 128),), jnp.float32),
        "weights": normal_values(streams_of[1], (R, NPTS), 0.02, 0.12, ((1, 128),), jnp.float32),
        "interp": normal_values(streams_of[2], (NLEAF, LEAF, SK), LEAF ** -0.5, 0.25, ((0, 128),), jnp.float32),
        "transfer": normal_values(streams_of[3], (NODES_UP, 2 * SK, SK), (2 * SK) ** -0.5, 0.25, (), jnp.float32),
        "near_count": jax.vmap(lambda own: ragged_sizes(own, LG, NEAR_MEAN * LG, NEAR, 2))(jax.random.split(streams_of[4], GROUPS)).reshape((GROUPS, LG)).astype(jnp.int32),
        "near_src": draw_near_src(jax.random.fold_in(streams_of[9], 71), 0),
        "skel_group": draw_skel_group(jax.random.fold_in(streams_of[9], 71), 0),
        "skel_node": draw_skel_node(jax.random.fold_in(streams_of[9], 71), 0),
        "far_nodes": draw_far_nodes(jax.random.fold_in(streams_of[9], 71), 0),
    }


HIGH = lax.Precision.HIGHEST


def kernel_block(source, target):
    cross = lax.dot_general(source, target, (((0,), (0,)), ((), ())), precision=HIGH, preferred_element_type=jnp.float32)
    source_sq = jnp.sum(source * source, axis=0)
    target_sq = jnp.sum(target * target, axis=0)
    dist = source_sq[:, None] + target_sq[None, :] - 2.0 * cross
    return jnp.exp((0.5 * F - dist) * 0.25)


def apply_block(source_pts, source_vals, target_pts):
    return jnp.dot(source_vals, kernel_block(source_pts, target_pts), precision=HIGH, preferred_element_type=jnp.float32)


def take_columns(cols, index):
    return jnp.take(cols, index, axis=1)


def reference(points, weights, interp, transfer, near_count, near_src, skel_group, skel_node, far_nodes):
    groups = GROUPS
    levels = groups.bit_length() - 1
    leaf_vals = weights.reshape(R, NLEAF, LEAF)
    leaf_up = jnp.einsum('rjl,jls->jrs', leaf_vals, interp, precision=HIGH)
    group_up = jnp.sum(leaf_up.reshape(groups, LG, R, SK), axis=1)
    group_pts = points.reshape(F, groups, LG * LEAF)
    group_skel = jax.vmap(take_columns, in_axes=(1, 0))(group_pts, skel_group)
    tier_pts = [group_skel]
    tier_vals = [group_up]
    row = 0
    for level in range(1, levels):
        count = groups >> level
        prev_pts = tier_pts[-1].reshape(count, 2, F, SK)
        prev_vals = tier_vals[-1].reshape(count, 2, R, SK)
        both_pts = jnp.concatenate([prev_pts[:, 0], prev_pts[:, 1]], axis=2)
        both_vals = jnp.concatenate([prev_vals[:, 0], prev_vals[:, 1]], axis=2)
        chosen = jax.vmap(take_columns)(both_pts, skel_node[row:row + count])
        merged = jnp.einsum('nrc,ncs->nrs', both_vals, transfer[row:row + count], precision=HIGH)
        tier_pts.append(chosen)
        tier_vals.append(merged)
        row += count
    far_parts = []
    start = 0
    for level in range(levels):
        count = groups >> level
        lists = far_nodes[start:start + count]
        pts = tier_pts[level]
        vals = tier_vals[level]

        def node_far(target, ids, pts=pts, vals=vals):
            total = jnp.zeros((R, SK), jnp.float32)
            for slot in range(FL):
                total = total + apply_block(pts[ids[slot]], vals[ids[slot]], target)
            return total

        far_parts.append(jax.vmap(node_far)(pts, lists))
        start += count
    local = far_parts[levels - 1]
    row = NODES_UP
    for level in range(levels - 1, 0, -1):
        count = groups >> level
        row -= count
        pushed = jnp.einsum('nrs,ncs->nrc', local, transfer[row:row + count], precision=HIGH)
        split = pushed.reshape(count, R, 2, SK).transpose(0, 2, 1, 3).reshape(2 * count, R, SK)
        local = far_parts[level - 1] + split
    far_out = jnp.einsum('grs,gjls->rgjl', local, interp.reshape(groups, LG, LEAF, SK), precision=HIGH).reshape(R, NPTS)
    counts = near_count.reshape(NLEAF)

    def leaf_near(inputs):
        leaf, count, sources = inputs
        target = lax.dynamic_slice_in_dim(points, leaf * LEAF, LEAF, 1)

        def one(slot, total):
            src = sources[slot]
            src_pts = lax.dynamic_slice_in_dim(points, src * LEAF, LEAF, 1)
            src_vals = lax.dynamic_slice_in_dim(weights, src * LEAF, LEAF, 1)
            term = apply_block(src_pts, src_vals, target)
            return total + jnp.where(slot < count, term, jnp.zeros_like(term))

        return lax.fori_loop(0, NEAR, one, jnp.zeros((R, LEAF), jnp.float32))

    near = lax.map(leaf_near, (jnp.arange(NLEAF, dtype=jnp.int32), counts, near_src))
    near_out = near.transpose(1, 0, 2).reshape(R, NPTS)
    return far_out + near_out
```

```python
import jax
import jax.numpy as jnp
from jax import lax
from jax.experimental import pallas as pl
from jax.experimental.pallas import tpu as pltpu
from jax.sharding import PartitionSpec as P

F = 64
R = 256
LEAF = 512
SK = 256
NEAR = 32
GROUPS = 16
HELP = 8
OWN = 2
COLS = OWN * LEAF
XS = 4
LEVELS = 4
UPPER = 14
STARTS = (0, 16, 24, 28)
NODES = 30
ROWS = R // HELP
PROWS = F // HELP
PACK = ROWS + PROWS
PARTS = 1 + R // F
ROOT_HALF = 0.7071067811865476

BF = jnp.bfloat16
F32 = jnp.float32
MESH = pl.DeviceIdType.MESH


def halves(value):
    high = value.astype(BF)
    return high, (value - high.astype(F32)).astype(BF)


def mul(left, right):
    return jnp.dot(left, right, preferred_element_type=F32)


def mul_t(left, right):
    return lax.dot_general(left, right, (((1,), (1,)), ((), ())), preferred_element_type=F32)


def product3(left, right, dot=mul):
    left_hi, left_lo = halves(left)
    right_hi, right_lo = halves(right)
    return dot(left_hi, right_hi) + dot(left_lo, right_hi) + dot(left_hi, right_lo)


def stacked_halves(pts):
    scaled = pts * ROOT_HALF
    high = scaled.astype(BF).astype(F32)
    low = (scaled - high).astype(BF).astype(F32)
    return jnp.concatenate([high, low], axis=0)


def target_side(both):
    high, low = both[:F], both[F:]
    whole = high + low
    own = 4.0 - 0.5 * jnp.sum(whole * whole, axis=0, keepdims=True)
    high, low = high.astype(BF), low.astype(BF)
    return jnp.concatenate([high, high, low, low], axis=0), own


def source_side(both):
    turned = both.T
    whole = turned[:, :F] + turned[:, F:]
    own = 4.0 - 0.5 * jnp.sum(whole * whole, axis=1, keepdims=True)
    turned = turned.astype(BF)
    return jnp.concatenate([turned, turned], axis=1), own


def remote(src, dst, send, recv, group, helper):
    return pltpu.make_async_remote_copy(
        src_ref=src,
        dst_ref=dst,
        send_sem=send,
        recv_sem=recv,
        device_id=(group, helper),
        device_id_type=MESH,
    )


def spread_kernel(
    pts, wts, interp, transfer, skg, skn, far, meta,
    cloud, tgt, metas, far_out,
    tr, rs_send, rs_buf, lf_send, lf_buf, p_send, p_buf, tier_u, tier_z, v_buf,
    load_sem, y_send, y_recv, f_send, f_recv, s_send, s_recv, own_sem,
    t_send, t_recv, m_send, m_recv, rs_ss, rs_rs, lf_ss, lf_rs, p_ss, p_rs, v_ss, v_rs,
):
    g = lax.axis_index("leaf")
    h = lax.axis_index("help")
    x = lax.div(h, 2)
    core = lax.rem(h, 2)
    sib = h + 1 - 2 * core
    after = lax.rem(g + 1, GROUPS)
    before = lax.rem(g + GROUPS - 1, GROUPS)

    def helper_at(d):
        return lax.rem(h + d, HELP)

    def group_at(d):
        return lax.rem(g + d, GROUPS)

    load = pltpu.make_async_copy(transfer, tr, load_sem)
    load.start()

    barrier = pltpu.get_barrier_semaphore()

    @pl.loop(1, HELP)
    def _(d):
        pl.semaphore_signal(barrier, inc=1, device_id=(g, helper_at(d)), device_id_type=MESH)

    @pl.loop(1, GROUPS)
    def _(d):
        pl.semaphore_signal(barrier, inc=1, device_id=(group_at(d), h), device_id_type=MESH)

    pl.semaphore_wait(barrier, HELP + GROUPS - 2)

    def part(i):
        return pts if i == 0 else wts.at[pl.ds(F * (i - 1), F)]

    def y_copy(way, i):
        where = after if way == 0 else before
        return remote(
            part(i), cloud.at[2 * way, core, i], y_send.at[way, i], y_recv.at[way, i], where, h
        )

    def f_copy(way, i):
        spot = cloud.at[2 * way, core, i]
        return remote(spot, spot, f_send.at[way, i], f_recv.at[way, i], g, sib)

    def s_copy(i):
        return remote(part(i), cloud.at[1, core, i], s_send.at[i], s_recv.at[i], g, sib)

    def own_copy(i):
        return pltpu.make_async_copy(part(i), cloud.at[1, core, i], own_sem.at[i])

    def x_at(d):
        return lax.rem(x + d, XS) * 2 + core

    def t_copy(d):
        return remote(pts, tgt.at[x], t_send.at[d], t_recv.at[d], g, x_at(d))

    def m_copy(d):
        return remote(meta, metas.at[x], m_send.at[d], m_recv.at[d], g, x_at(d))

    own_t = pltpu.make_async_copy(pts, tgt.at[x], own_sem.at[PARTS])
    own_m = pltpu.make_async_copy(meta, metas.at[x], own_sem.at[PARTS + 1])

    for i in range(PARTS):
        y_copy(0, i).start()
        y_copy(1, i).start()

    picks = skg[...] - h * COLS
    onehot = (lax.broadcasted_iota(jnp.int32, (COLS, SK), 0) == picks).astype(BF)
    own_pts = pts[...]
    first, rest = halves(own_pts)
    second = (own_pts - first.astype(F32)).astype(BF)
    third = (own_pts - first.astype(F32) - second.astype(F32)).astype(BF)
    del rest
    chosen = mul(first, onehot) + mul(second, onehot) + mul(third, onehot)
    up = product3(wts[...], interp[...].reshape(COLS, SK))
    rs_send[:, :ROWS, :] = up.reshape(HELP, ROWS, SK)
    rs_send[:, ROWS:, :] = chosen.reshape(HELP, PROWS, SK)

    def rs_copy(d):
        to = helper_at(d)
        return remote(rs_send.at[to], rs_buf.at[h], rs_ss.at[d], rs_rs.at[d], g, to)

    @pl.loop(1, HELP)
    def _(d):
        rs_copy(d).start()

    for d in range(1, XS):
        t_copy(d).start()
        m_copy(d).start()
    for i in range(PARTS):
        s_copy(i).start()
        own_copy(i).start()
    own_t.start()
    own_m.start()

    @pl.loop(1, HELP)
    def _(d):
        rs_copy(d).wait_recv()

    rs_buf[h] = rs_send[h]
    total = rs_buf[0]
    for i in range(1, HELP):
        total = total + rs_buf[i]
    lf_send[...] = total

    def lf_copy(d):
        return remote(lf_send, lf_buf.at[g], lf_ss.at[d], lf_rs.at[d], group_at(d), h)

    @pl.loop(1, GROUPS)
    def _(d):
        lf_copy(d).start()

    lf_buf[g] = total
    load.wait()

    @pl.loop(1, GROUPS)
    def _(d):
        lf_copy(d).wait_recv()

    p_send[...] = lf_buf[:, ROWS:, :]

    def p_copy(d):
        return remote(p_send, p_buf.at[h], p_ss.at[d], p_rs.at[d], g, helper_at(d))

    @pl.loop(1, HELP)
    def _(d):
        p_copy(d).start()

    p_buf[h] = p_send[...]

    tier_u[:GROUPS] = lf_buf[:, :ROWS, :]

    @pl.loop(0, UPPER)
    def _(r):
        both = jnp.concatenate([tier_u[2 * r], tier_u[2 * r + 1]], axis=1)
        tier_u[GROUPS + r] = product3(both, tr[r])

    @pl.loop(1, HELP)
    def _(d):
        p_copy(d).wait_recv()

    @pl.loop(0, GROUPS)
    def _(n):
        tier_z[n] = stacked_halves(p_buf[:, n].reshape(F, SK)).astype(BF)

    rows = lax.broadcasted_iota(jnp.int32, (2 * SK, SK), 0)

    @pl.loop(0, UPPER)
    def _(r):
        both = jnp.concatenate([tier_z[2 * r], tier_z[2 * r + 1]], axis=1)
        pick = (rows == skn[pl.ds(r, 1), :]).astype(BF)
        tier_z[GROUPS + r] = mul(both, pick).astype(BF)

    sums = []
    for level in range(LEVELS):
        q = STARTS[level] + lax.shift_right_logical(g, level)
        right, target_own = target_side(tier_z[q].astype(F32))

        def one(slot, acc, level=level, q=q, right=right, target_own=target_own):
            node = STARTS[level] + far[q, slot]
            left, source_own = source_side(tier_z[node].astype(F32))
            block = jnp.exp(mul(left, right) + source_own + target_own)
            return acc + product3(tier_u[node], block)

        sums.append(lax.fori_loop(0, 4, one, jnp.zeros((ROWS, SK), F32)))

    local = sums[LEVELS - 1]
    for level in range(LEVELS - 1, 0, -1):
        r = STARTS[level] - GROUPS + lax.shift_right_logical(g, level)
        side = lax.rem(lax.shift_right_logical(g, level - 1), 2)
        half = tr[r, pl.ds(pl.multiple_of(side * SK, SK), SK), :]
        local = sums[level - 1] + product3(local, half, mul_t)
    v_buf[h] = local

    def v_copy(d):
        return remote(v_buf.at[h], v_buf.at[h], v_ss.at[d], v_rs.at[d], g, helper_at(d))

    @pl.loop(1, HELP)
    def _(d):
        v_copy(d).start()

    for i in range(PARTS):
        for way in range(2):
            y_copy(way, i).wait_recv()
            f_copy(way, i).start()

    @pl.loop(1, HELP)
    def _(d):
        v_copy(d).wait_recv()

    far_out[...] = product3(v_buf[...].reshape(R, SK), interp[...].reshape(COLS, SK), mul_t)

    for i in range(PARTS):
        for way in range(2):
            f_copy(way, i).wait()
            y_copy(way, i).wait_send()
        s_copy(i).wait()
        own_copy(i).wait()
    for d in range(1, XS):
        t_copy(d).wait()
        m_copy(d).wait()
    own_t.wait()
    own_m.wait()

    @pl.loop(1, HELP)
    def _(d):
        rs_copy(d).wait_send()
        p_copy(d).wait_send()
        v_copy(d).wait_send()

    @pl.loop(1, GROUPS)
    def _(d):
        lf_copy(d).wait_send()


def spread(points, weights, interp, transfer, skel_group, skel_node, far_nodes, meta):
    vmem = pl.BlockSpec(memory_space=pltpu.VMEM)
    smem = pl.BlockSpec(memory_space=pltpu.SMEM)
    anym = pl.BlockSpec(memory_space=pl.ANY)
    dma = pltpu.SemaphoreType.DMA
    return pl.pallas_call(
        spread_kernel,
        out_shape=(
            jax.ShapeDtypeStruct((3, 2, PARTS, F, COLS), F32),
            jax.ShapeDtypeStruct((XS, F, COLS), F32),
            jax.ShapeDtypeStruct((XS, 8, 128), jnp.int32),
            jax.ShapeDtypeStruct((R, COLS), F32),
        ),
        in_specs=[vmem, vmem, vmem, anym, vmem, vmem, smem, vmem],
        out_specs=(anym, anym, anym, vmem),
        scratch_shapes=[
            pltpu.VMEM((UPPER, 2 * SK, SK), F32),
            pltpu.VMEM((HELP, PACK, SK), F32),
            pltpu.VMEM((HELP, PACK, SK), F32),
            pltpu.VMEM((PACK, SK), F32),
            pltpu.VMEM((GROUPS, PACK, SK), F32),
            pltpu.VMEM((GROUPS, PROWS, SK), F32),
            pltpu.VMEM((HELP, GROUPS, PROWS, SK), F32),
            pltpu.VMEM((NODES, ROWS, SK), F32),
            pltpu.VMEM((NODES, 2 * F, SK), BF),
            pltpu.VMEM((HELP, ROWS, SK), F32),
            dma,
            dma((2, PARTS)), dma((2, PARTS)),
            dma((2, PARTS)), dma((2, PARTS)),
            dma((PARTS,)), dma((PARTS,)),
            dma((PARTS + 2,)),
            dma((XS,)), dma((XS,)),
            dma((XS,)), dma((XS,)),
            dma((HELP,)), dma((HELP,)),
            dma((GROUPS,)), dma((GROUPS,)),
            dma((HELP,)), dma((HELP,)),
            dma((HELP,)), dma((HELP,)),
        ],
        compiler_params=pltpu.CompilerParams(
            collective_id=0, has_side_effects=True, vmem_limit_bytes=40 << 20
        ),
        name="spread",
    )(points, weights, interp, transfer, skel_group, skel_node, far_nodes, meta)


SRC = 3 * 2 * OWN
TGT = XS * OWN


def near_kernel(times, logs, cloud, tgt, part, w_hi, w_lo, left, source_own, right, target_own):
    @pl.loop(0, 6)
    def _(pair):
        step, core = lax.div(pair, 2), lax.rem(pair, 2)
        for j in range(OWN):
            span = slice(j * LEAF, (j + 1) * LEAF)
            s = pair * OWN + j
            for i in range(R // F):
                high, low = halves(cloud[step, core, 1 + i, :, span])
                w_hi[s, i * F:(i + 1) * F, :] = high
                w_lo[s, i * F:(i + 1) * F, :] = low
            factor, own = source_side(stacked_halves(cloud[step, core, 0, :, span]))
            left[s] = factor
            source_own[s] = jnp.broadcast_to(own, (LEAF, 128))

    @pl.loop(0, XS)
    def _(at):
        for j in range(OWN):
            factor, own = target_side(stacked_halves(tgt[at, :, j * LEAF:(j + 1) * LEAF]))
            right[at * OWN + j] = factor
            target_own[at * OWN + j] = jnp.broadcast_to(own, (8, LEAF))

    @pl.loop(0, XS)
    def _(at):
        for j in range(OWN):
            t = at * OWN + j
            part[at, :, j * LEAF:(j + 1) * LEAF] = jnp.zeros((R, LEAF), F32)

            @pl.loop(0, SRC)
            def _(s, t=t, j=j):
                @pl.when(times[t * SRC + s] > 0)
                def _():
                    log = logs[t * SRC + s]
                    own = source_own[s]
                    for c in range(2):
                        span = slice(c * 256, (c + 1) * 256)
                        cross = mul(left[s], right[t, :, span])
                        shift = target_own[t, 0:1, span] + log
                        block = jnp.exp(cross + jnp.concatenate([own, own], axis=1) + shift)
                        high, low = halves(block)
                        where = slice(j * LEAF + c * 256, j * LEAF + (c + 1) * 256)
                        part[at, :, where] += (
                            mul(w_hi[s], high) + mul(w_lo[s], high) + mul(w_hi[s], low)
                        )


def near(times, logs, cloud, tgt):
    vmem = pl.BlockSpec(memory_space=pltpu.VMEM)
    smem = pl.BlockSpec(memory_space=pltpu.SMEM)
    return pl.pallas_call(
        near_kernel,
        out_shape=jax.ShapeDtypeStruct((XS, R, COLS), F32),
        in_specs=[smem, smem, vmem, vmem],
        out_specs=vmem,
        scratch_shapes=[
            pltpu.VMEM((SRC, R, LEAF), BF),
            pltpu.VMEM((SRC, R, LEAF), BF),
            pltpu.VMEM((SRC, LEAF, 4 * F), BF),
            pltpu.VMEM((SRC, LEAF, 128), F32),
            pltpu.VMEM((TGT, 4 * F, LEAF), BF),
            pltpu.VMEM((TGT, 8, LEAF), F32),
        ],
        compiler_params=pltpu.CompilerParams(vmem_limit_bytes=48 << 20),
        name="near",
    )(times, logs, cloud, tgt)


HALF = R // 2


def fold_kernel(part, far_out, out, first, last, first_ss, first_rs, last_ss, last_rs):
    g = lax.axis_index("leaf")
    h = lax.axis_index("help")
    x = lax.div(h, 2)
    core = lax.rem(h, 2)

    def x_at(d):
        return lax.rem(x + d, XS)

    def to(way):
        return x_at(1 if way == 0 else 3) * 2 + core

    barrier = pltpu.get_barrier_semaphore()
    for way in range(2):
        pl.semaphore_signal(barrier, inc=1, device_id=(g, to(way)), device_id_type=MESH)
    pl.semaphore_wait(barrier, 2)

    def rows(i):
        return pl.ds(i * HALF, HALF)

    def first_copy(way):
        src = part.at[x_at(2), rows(way)]
        return remote(src, first.at[way], first_ss.at[way], first_rs.at[way], g, to(way))

    def plain_copy(way):
        src = part.at[x_at(1 if way == 0 else 3), rows(1 - way)]
        dst = last.at[way, rows(1 - way)]
        return remote(src, dst, last_ss.at[way, 0], last_rs.at[way, 0], g, to(way))

    def sum_copy(way):
        dst = last.at[way, rows(way)]
        return remote(first.at[way], dst, last_ss.at[way, 1], last_rs.at[way, 1], g, to(way))

    for way in range(2):
        first_copy(way).start()
    for way in range(2):
        plain_copy(way).start()
    out[...] = far_out[...] + part[x]
    for way in range(2):
        first_copy(way).wait_recv()
        first[way] += part[x_at(1 if way == 0 else 3), rows(way), :]
        sum_copy(way).start()
    for way in range(2):
        plain_copy(way).wait_recv()
    out[rows(1), :] += last[0, rows(1), :]
    out[rows(0), :] += last[1, rows(0), :]
    for way in range(2):
        sum_copy(way).wait_recv()
    out[rows(0), :] += last[0, rows(0), :]
    out[rows(1), :] += last[1, rows(1), :]
    for way in range(2):
        first_copy(way).wait_send()
        plain_copy(way).wait_send()
        sum_copy(way).wait_send()


def fold(part, far_out):
    vmem = pl.BlockSpec(memory_space=pltpu.VMEM)
    dma = pltpu.SemaphoreType.DMA
    return pl.pallas_call(
        fold_kernel,
        out_shape=jax.ShapeDtypeStruct((R, COLS), F32),
        in_specs=[vmem, vmem],
        out_specs=vmem,
        scratch_shapes=[
            pltpu.VMEM((2, HALF, COLS), F32),
            pltpu.VMEM((2, R, COLS), F32),
            dma((2,)), dma((2,)), dma((2, 2)), dma((2, 2)),
        ],
        compiler_params=pltpu.CompilerParams(
            collective_id=1, has_side_effects=True, vmem_limit_bytes=24 << 20
        ),
        name="fold",
    )(part, far_out)


def shards(
    points, weights, interp, transfer, near_count, near_src, skel_group, skel_node, far_nodes
):
    g = lax.axis_index("leaf")
    x = lax.axis_index("help") // 2
    listed = jnp.where(lax.iota(jnp.int32, NEAR)[None, :] < near_count[0][:, None], near_src, -1)
    meta = jnp.pad(listed, ((0, 8 - OWN), (0, 128 - NEAR)), constant_values=-1)
    cloud, tgt, metas, far_out = spread(
        points, weights, interp, transfer, skel_group, skel_node, far_nodes, meta
    )
    slots = metas[:, :OWN, :NEAR].reshape(TGT, 1, NEAR)
    step = lax.iota(jnp.int32, SRC)
    ids = (g - 1 + step // 4) * 16 + x * 4 + step % 4
    ids = jnp.where(ids < 0, -2, ids)
    times = jnp.sum((slots == ids[None, :, None]).astype(jnp.int32), axis=2).reshape(-1)
    logs = jnp.log(jnp.maximum(times, 1).astype(F32))
    part = near(times, logs, cloud, tgt)
    return fold(part, far_out)


def solution(mesh):
    placed = (
        P(None, ("leaf", "help")),
        P(None, ("leaf", "help")),
        P(("leaf", "help"), None, None),
        P(),
        P("leaf", "help"),
        P(("leaf", "help"), None),
        P("leaf", None),
        P(),
        P(),
    )
    return jax.shard_map(
        shards, mesh=mesh, in_specs=placed, out_specs=P(None, ("leaf", "help")), check_vma=False
    )
```

```python
import jax
import jax.numpy as jnp
from jax import lax
from jax.experimental import pallas as pl
from jax.experimental.pallas import tpu as pltpu
from jax.sharding import PartitionSpec as P

F = 64
R = 256
LEAF = 512
SK = 256
NEAR = 32
GROUPS = 16
HELP = 8
OWN = 2
COLS = OWN * LEAF
XS = 4
LEVELS = 4
UPPER = 14
STARTS = (0, 16, 24, 28)
NODES = 30
ROWS = R // HELP
PROWS = F // HELP
PARTS = 1 + R // F
ROOT = 0.8493218002880191
PEAK = 5.770780163555854

BF = jnp.bfloat16
F32 = jnp.float32
MESH = pl.DeviceIdType.MESH


def halves(value):
    high = value.astype(BF)
    return high, (value - high.astype(F32)).astype(BF)


def mul(left, right):
    return jnp.dot(left, right, preferred_element_type=F32)


def mul_t(left, right):
    return lax.dot_general(left, right, (((1,), (1,)), ((), ())), preferred_element_type=F32)


def product3(left, right, dot=mul):
    left_hi, left_lo = halves(left)
    right_hi, right_lo = halves(right)
    return dot(left_hi, right_hi) + dot(left_lo, right_hi) + dot(left_hi, right_lo)


def stacked_halves(pts):
    scaled = pts * ROOT
    high = scaled.astype(BF).astype(F32)
    low = (scaled - high).astype(BF).astype(F32)
    return jnp.concatenate([high, low], axis=0)


def target_side(both):
    high, low = both[:F], both[F:]
    whole = high + low
    own = PEAK - 0.5 * jnp.sum(whole * whole, axis=0, keepdims=True)
    high, low = high.astype(BF), low.astype(BF)
    return jnp.concatenate([high, high, low, low], axis=0), own


def source_side(both):
    turned = both.T
    whole = turned[:, :F] + turned[:, F:]
    own = PEAK - 0.5 * jnp.sum(whole * whole, axis=1, keepdims=True)
    turned = turned.astype(BF)
    return jnp.concatenate([turned, turned], axis=1), own


def remote(src, dst, send, recv, group, helper):
    return pltpu.make_async_remote_copy(
        src_ref=src,
        dst_ref=dst,
        send_sem=send,
        recv_sem=recv,
        device_id=(group, helper),
        device_id_type=MESH,
    )


def spread_kernel(
    pts, wts, interp, transfer, skg, skn, far, meta,
    cloud, tgt, metas, far_out,
    pts_v, wts_v, int_v, tr, skg_v, skn_v, far_s,
    ps_send, ps_buf, us_send, us_buf, lp_send, lp_buf, lu_send, p_buf, tier_u, tier_z, v_buf,
    load_sem, y_send, y_recv, f_send, f_recv, s_send, s_recv, own_sem,
    t_send, t_recv, m_send, m_recv,
    ps_ss, ps_rs, us_ss, us_rs, lp_ss, lp_rs, lu_ss, lu_rs, p_ss, p_rs, v_ss, v_rs,
):
    g = lax.axis_index("leaf")
    h = lax.axis_index("help")
    x = lax.div(h, 2)
    core = lax.rem(h, 2)
    sib = h + 1 - 2 * core
    after = lax.rem(g + 1, GROUPS)
    before = lax.rem(g + GROUPS - 1, GROUPS)

    def helper_at(d):
        return lax.rem(h + d, HELP)

    def group_at(d):
        return lax.rem(g + d, GROUPS)

    barrier = pltpu.get_barrier_semaphore()

    @pl.loop(1, HELP)
    def _(d):
        pl.semaphore_signal(barrier, inc=1, device_id=(g, helper_at(d)), device_id_type=MESH)

    @pl.loop(1, GROUPS)
    def _(d):
        pl.semaphore_signal(barrier, inc=1, device_id=(group_at(d), h), device_id_type=MESH)

    pairs = (
        (pts, pts_v), (skg, skg_v), (wts, wts_v), (interp, int_v),
        (far, far_s), (skn, skn_v), (transfer, tr),
    )
    loads = [
        pltpu.make_async_copy(src, dst, load_sem.at[i]) for i, (src, dst) in enumerate(pairs)
    ]
    for copy in loads:
        copy.start()

    def part(i):
        return pts if i == 0 else wts.at[pl.ds(F * (i - 1), F)]

    def y_copy(way, i):
        where = after if way == 0 else before
        return remote(
            part(i), cloud.at[2 * way, core, i], y_send.at[way, i], y_recv.at[way, i], where, h
        )

    def f_copy(way, i):
        spot = cloud.at[2 * way, core, i]
        return remote(spot, spot, f_send.at[way, i], f_recv.at[way, i], g, sib)

    sends = (g < GROUPS - 1, g > 0)

    def y_start(i):
        for way in range(2):
            pl.when(sends[way])(y_copy(way, i).start)

    def f_start(i):
        for way in range(2):

            @pl.when(sends[1 - way])
            def _(way=way):
                y_copy(way, i).wait_recv()
                f_copy(way, i).start()

    def s_copy(i):
        return remote(part(i), cloud.at[1, core, i], s_send.at[i], s_recv.at[i], g, sib)

    def own_copy(i):
        src = pts_v if i == 0 else wts_v.at[pl.ds(F * (i - 1), F)]
        return pltpu.make_async_copy(src, cloud.at[1, core, i], own_sem.at[i])

    def x_at(d):
        return lax.rem(x + d, XS) * 2 + core

    def t_copy(d):
        return remote(pts, tgt.at[x], t_send.at[d], t_recv.at[d], g, x_at(d))

    def m_copy(d):
        return remote(meta, metas.at[x], m_send.at[d], m_recv.at[d], g, x_at(d))

    own_t = pltpu.make_async_copy(pts_v, tgt.at[x], own_sem.at[PARTS])
    own_m = pltpu.make_async_copy(meta, metas.at[x], own_sem.at[PARTS + 1])

    loads[0].wait()
    loads[1].wait()
    picks = skg_v[...] - h * COLS
    onehot = (lax.broadcasted_iota(jnp.int32, (COLS, SK), 0) == picks).astype(BF)
    own_pts = pts_v[...]
    first = own_pts.astype(BF)
    rest = own_pts - first.astype(F32)
    second, third = halves(rest)
    chosen = mul(first, onehot) + mul(second, onehot) + mul(third, onehot)
    ps_send[...] = chosen.reshape(HELP, PROWS, SK)

    pl.semaphore_wait(barrier, HELP + GROUPS - 2)

    def ps_copy(d):
        to = helper_at(d)
        return remote(ps_send.at[to], ps_buf.at[h], ps_ss.at[d], ps_rs.at[d], g, to)

    def us_copy(d):
        to = helper_at(d)
        return remote(us_send.at[to], us_buf.at[h], us_ss.at[d], us_rs.at[d], g, to)

    def lp_copy(d):
        return remote(lp_send, lp_buf.at[g], lp_ss.at[d], lp_rs.at[d], group_at(d), h)

    def lu_copy(d):
        return remote(lu_send, tier_u.at[g], lu_ss.at[d], lu_rs.at[d], group_at(d), h)

    def p_copy(d):
        return remote(lp_buf, p_buf.at[h], p_ss.at[d], p_rs.at[d], g, helper_at(d))

    def v_copy(d):
        return remote(v_buf.at[h], v_buf.at[h], v_ss.at[d], v_rs.at[d], g, helper_at(d))

    @pl.loop(1, HELP)
    def _(d):
        ps_copy(d).start()

    y_start(0)

    loads[2].wait()
    loads[3].wait()
    up = product3(wts_v[...], int_v[...].reshape(COLS, SK))
    us_send[...] = up.reshape(HELP, ROWS, SK)

    @pl.loop(1, HELP)
    def _(d):
        us_copy(d).start()

    y_start(1)

    @pl.loop(1, HELP)
    def _(d):
        ps_copy(d).wait_recv()

    ps_buf[h] = ps_send[h]
    total = ps_buf[0]
    for i in range(1, HELP):
        total = total + ps_buf[i]
    lp_send[...] = total
    lp_buf[g] = total

    @pl.loop(1, GROUPS)
    def _(d):
        lp_copy(d).start()

    @pl.loop(1, HELP)
    def _(d):
        us_copy(d).wait_recv()

    us_buf[h] = us_send[h]
    total = us_buf[0]
    for i in range(1, HELP):
        total = total + us_buf[i]
    lu_send[...] = total
    tier_u[g] = total

    @pl.loop(1, GROUPS)
    def _(d):
        lu_copy(d).start()

    y_start(2)

    @pl.loop(1, GROUPS)
    def _(d):
        lp_copy(d).wait_recv()

    @pl.loop(1, HELP)
    def _(d):
        p_copy(d).start()

    p_buf[h] = lp_buf[...]
    for d in range(1, XS):
        t_copy(d).start()
        m_copy(d).start()
    for i in range(PARTS):
        s_copy(i).start()
        own_copy(i).start()
    own_t.start()
    own_m.start()

    @pl.loop(1, GROUPS)
    def _(d):
        lu_copy(d).wait_recv()

    y_start(3)
    y_start(4)

    for copy in loads[4:]:
        copy.wait()

    @pl.loop(0, UPPER, unroll=2)
    def _(r):
        both = jnp.concatenate([tier_u[2 * r], tier_u[2 * r + 1]], axis=1)
        tier_u[GROUPS + r] = product3(both, tr[r])

    f_start(0)

    @pl.loop(1, HELP)
    def _(d):
        p_copy(d).wait_recv()

    @pl.loop(0, GROUPS)
    def _(n):
        tier_z[n] = stacked_halves(p_buf[:, n].reshape(F, SK)).astype(BF)

    rows = lax.broadcasted_iota(jnp.int32, (2 * SK, SK), 0)

    @pl.loop(0, UPPER, unroll=2)
    def _(r):
        both = jnp.concatenate([tier_z[2 * r], tier_z[2 * r + 1]], axis=1)
        pick = (rows == skn_v[pl.ds(r, 1), :]).astype(BF)
        tier_z[GROUPS + r] = mul(both, pick).astype(BF)

    f_start(1)
    sums = []
    for level in range(LEVELS):
        q = STARTS[level] + lax.shift_right_logical(g, level)
        right, target_own = target_side(tier_z[q].astype(F32))
        nodes = [STARTS[level] + far_s[q, slot] for slot in range(4)]
        both = jnp.concatenate([tier_z[node] for node in nodes], axis=1).astype(F32)
        left, source_own = source_side(both)
        block = jnp.exp2(mul(left, right) + source_own + target_own)
        values = jnp.concatenate([tier_u[node] for node in nodes], axis=1)
        sums.append(product3(values, block))

    f_start(2)
    local = sums[LEVELS - 1]
    for level in range(LEVELS - 1, 0, -1):
        r = STARTS[level] - GROUPS + lax.shift_right_logical(g, level)
        side = lax.rem(lax.shift_right_logical(g, level - 1), 2)
        half = tr[r, pl.ds(pl.multiple_of(side * SK, SK), SK), :]
        local = sums[level - 1] + product3(local, half, mul_t)
    v_buf[h] = local

    @pl.loop(1, HELP)
    def _(d):
        v_copy(d).start()

    f_start(3)
    f_start(4)

    @pl.loop(1, HELP)
    def _(d):
        v_copy(d).wait_recv()

    far_out[...] = product3(v_buf[...].reshape(R, SK), int_v[...].reshape(COLS, SK), mul_t)

    for i in range(PARTS):
        for way in range(2):
            pl.when(sends[1 - way])(f_copy(way, i).wait)
            pl.when(sends[way])(y_copy(way, i).wait_send)
        s_copy(i).wait()
        own_copy(i).wait()
    for d in range(1, XS):
        t_copy(d).wait()
        m_copy(d).wait()
    own_t.wait()
    own_m.wait()

    @pl.loop(1, HELP)
    def _(d):
        ps_copy(d).wait_send()
        us_copy(d).wait_send()
        p_copy(d).wait_send()
        v_copy(d).wait_send()

    @pl.loop(1, GROUPS)
    def _(d):
        lp_copy(d).wait_send()
        lu_copy(d).wait_send()


def spread(points, weights, interp, transfer, skel_group, skel_node, far_nodes, meta):
    vmem = pl.BlockSpec(memory_space=pltpu.VMEM)
    anym = pl.BlockSpec(memory_space=pl.ANY)
    dma = pltpu.SemaphoreType.DMA
    return pl.pallas_call(
        spread_kernel,
        out_shape=(
            jax.ShapeDtypeStruct((3, 2, PARTS, F, COLS), F32),
            jax.ShapeDtypeStruct((XS, F, COLS), F32),
            jax.ShapeDtypeStruct((XS, 8, 128), jnp.int32),
            jax.ShapeDtypeStruct((R, COLS), F32),
        ),
        in_specs=[anym] * 8,
        out_specs=(anym, anym, anym, vmem),
        scratch_shapes=[
            pltpu.VMEM((F, COLS), F32),
            pltpu.VMEM((R, COLS), F32),
            pltpu.VMEM((OWN, LEAF, SK), F32),
            pltpu.VMEM((UPPER, 2 * SK, SK), F32),
            pltpu.VMEM((1, SK), jnp.int32),
            pltpu.VMEM((UPPER, SK), jnp.int32),
            pltpu.SMEM((NODES, 4), jnp.int32),
            pltpu.VMEM((HELP, PROWS, SK), F32),
            pltpu.VMEM((HELP, PROWS, SK), F32),
            pltpu.VMEM((HELP, ROWS, SK), F32),
            pltpu.VMEM((HELP, ROWS, SK), F32),
            pltpu.VMEM((PROWS, SK), F32),
            pltpu.VMEM((GROUPS, PROWS, SK), F32),
            pltpu.VMEM((ROWS, SK), F32),
            pltpu.VMEM((HELP, GROUPS, PROWS, SK), F32),
            pltpu.VMEM((NODES, ROWS, SK), F32),
            pltpu.VMEM((NODES, 2 * F, SK), BF),
            pltpu.VMEM((HELP, ROWS, SK), F32),
            dma((7,)),
            dma((2, PARTS)), dma((2, PARTS)),
            dma((2, PARTS)), dma((2, PARTS)),
            dma((PARTS,)), dma((PARTS,)),
            dma((PARTS + 2,)),
            dma((XS,)), dma((XS,)),
            dma((XS,)), dma((XS,)),
            dma((HELP,)), dma((HELP,)),
            dma((HELP,)), dma((HELP,)),
            dma((GROUPS,)), dma((GROUPS,)),
            dma((GROUPS,)), dma((GROUPS,)),
            dma((HELP,)), dma((HELP,)),
            dma((HELP,)), dma((HELP,)),
        ],
        compiler_params=pltpu.CompilerParams(
            collective_id=0, has_side_effects=True, vmem_limit_bytes=60 << 20
        ),
        name="spread",
    )(points, weights, interp, transfer, skel_group, skel_node, far_nodes, meta)


SRC = 3 * 2 * OWN
TGT = XS * OWN
CUT = 2


def near_kernel(
    times, logs, cloud, tgt, part,
    w_hl, left, source_own, right, target_own,
    list_t, list_s, list_log, hi_a, lo_a, hi_b, lo_b,
):
    @pl.loop(0, 6)
    def _(pair):
        step, core = lax.div(pair, 2), lax.rem(pair, 2)
        for j in range(OWN):
            span = slice(j * LEAF, (j + 1) * LEAF)
            s = pair * OWN + j
            for i in range(R // F):
                high, low = halves(cloud[step, core, 1 + i, :, span])
                w_hl[s, i * F:(i + 1) * F, :] = high
                w_hl[s, R + i * F:R + (i + 1) * F, :] = low
            factor, own = source_side(stacked_halves(cloud[step, core, 0, :, span]))
            left[s] = factor
            source_own[s] = jnp.broadcast_to(own, (LEAF, 128))

    @pl.loop(0, XS)
    def _(at):
        for j in range(OWN):
            factor, own = target_side(stacked_halves(tgt[at, :, j * LEAF:(j + 1) * LEAF]))
            right[at * OWN + j] = factor
            target_own[at * OWN + j] = jnp.broadcast_to(own, (8, LEAF))
            part[at * OWN + j] = jnp.zeros((R, LEAF), F32)

    def note(k, n):
        list_t[n] = lax.div(k, SRC)
        list_s[n] = lax.rem(k, SRC)
        list_log[n] = logs[k]
        return n + (times[k] > 0).astype(jnp.int32)

    count = lax.fori_loop(0, TGT * SRC, note, jnp.int32(0))
    for extra in range(2):
        list_t[count + extra] = 0
        list_s[count + extra] = 0
        list_log[count + extra] = jnp.float32(-1e30)

    def produce(i, hi, lo):
        t, s = list_t[i], list_s[i]
        shift = target_own[t, 0:1, :] + list_log[i]
        own = source_own[s]
        for c in range(CUT):
            n = LEAF // CUT
            span = slice(c * n, (c + 1) * n)
            cross = mul(left[s], right[t, :, span])
            block = jnp.exp2(cross + jnp.concatenate([own] * (n // 128), axis=1) + shift[:, span])
            high, low = halves(block)
            hi[:, span] = high
            lo[:, span] = low

    def consume(i, hi, lo):
        t, s = list_t[i], list_s[i]
        for c in range(CUT):
            n = LEAF // CUT
            span = slice(c * n, (c + 1) * n)
            two = mul(w_hl[s], hi[:, span])
            part[t, :, span] += two[:R] + two[R:] + mul(w_hl[s, :R], lo[:, span])

    produce(0, hi_a, lo_a)

    @pl.loop(0, lax.div(count + 1, 2))
    def _(k):
        produce(2 * k + 1, hi_b, lo_b)
        consume(2 * k, hi_a, lo_a)
        produce(jnp.minimum(2 * k + 2, count), hi_a, lo_a)
        consume(2 * k + 1, hi_b, lo_b)


def near(times, logs, cloud, tgt):
    vmem = pl.BlockSpec(memory_space=pltpu.VMEM)
    smem = pl.BlockSpec(memory_space=pltpu.SMEM)
    return pl.pallas_call(
        near_kernel,
        out_shape=jax.ShapeDtypeStruct((TGT, R, LEAF), F32),
        in_specs=[smem, smem, vmem, vmem],
        out_specs=vmem,
        scratch_shapes=[
            pltpu.VMEM((SRC, 2 * R, LEAF), BF),
            pltpu.VMEM((SRC, LEAF, 4 * F), BF),
            pltpu.VMEM((SRC, LEAF, 128), F32),
            pltpu.VMEM((TGT, 4 * F, LEAF), BF),
            pltpu.VMEM((TGT, 8, LEAF), F32),
            pltpu.SMEM((TGT * SRC + 2,), jnp.int32),
            pltpu.SMEM((TGT * SRC + 2,), jnp.int32),
            pltpu.SMEM((TGT * SRC + 2,), F32),
            pltpu.VMEM((LEAF, LEAF), BF),
            pltpu.VMEM((LEAF, LEAF), BF),
            pltpu.VMEM((LEAF, LEAF), BF),
            pltpu.VMEM((LEAF, LEAF), BF),
        ],
        compiler_params=pltpu.CompilerParams(vmem_limit_bytes=48 << 20),
        name="near",
    )(times, logs, cloud, tgt)


def fold_kernel(part, far_out, out, first, last, first_ss, first_rs, last_ss, last_rs):
    g = lax.axis_index("leaf")
    h = lax.axis_index("help")
    x = lax.div(h, 2)
    core = lax.rem(h, 2)

    def x_at(d):
        return lax.rem(x + d, XS)

    def beside(way):
        return x_at(1 if way == 0 else 3)

    def to(way):
        return beside(way) * 2 + core

    barrier = pltpu.get_barrier_semaphore()
    for way in range(2):
        pl.semaphore_signal(barrier, inc=1, device_id=(g, to(way)), device_id_type=MESH)
    pl.semaphore_wait(barrier, 2)

    def first_copy(way):
        src = part.at[x_at(2) * OWN + way]
        return remote(src, first.at[way], first_ss.at[way], first_rs.at[way], g, to(way))

    def plain_copy(way):
        src = part.at[beside(way) * OWN + 1 - way]
        dst = last.at[way, 1 - way]
        return remote(src, dst, last_ss.at[way, 0], last_rs.at[way, 0], g, to(way))

    def sum_copy(way):
        dst = last.at[way, way]
        return remote(first.at[way], dst, last_ss.at[way, 1], last_rs.at[way, 1], g, to(way))

    for way in range(2):
        first_copy(way).start()
    for way in range(2):
        plain_copy(way).start()
    spans = [slice(j * LEAF, (j + 1) * LEAF) for j in range(OWN)]
    for j in range(OWN):
        out[:, spans[j]] = far_out[:, spans[j]] + part[x * OWN + j]
    for way in range(2):
        first_copy(way).wait_recv()
        first[way] += part[beside(way) * OWN + way]
        sum_copy(way).start()
    for way in range(2):
        plain_copy(way).wait_recv()
        out[:, spans[1 - way]] += last[way, 1 - way]
    for way in range(2):
        sum_copy(way).wait_recv()
        out[:, spans[way]] += last[way, way]
    for way in range(2):
        first_copy(way).wait_send()
        plain_copy(way).wait_send()
        sum_copy(way).wait_send()


def fold(part, far_out):
    vmem = pl.BlockSpec(memory_space=pltpu.VMEM)
    dma = pltpu.SemaphoreType.DMA
    return pl.pallas_call(
        fold_kernel,
        out_shape=jax.ShapeDtypeStruct((R, COLS), F32),
        in_specs=[vmem, vmem],
        out_specs=vmem,
        scratch_shapes=[
            pltpu.VMEM((2, R, LEAF), F32),
            pltpu.VMEM((2, OWN, R, LEAF), F32),
            dma((2,)), dma((2,)), dma((2, 2)), dma((2, 2)),
        ],
        compiler_params=pltpu.CompilerParams(
            collective_id=1, has_side_effects=True, vmem_limit_bytes=24 << 20
        ),
        name="fold",
    )(part, far_out)


def shards(
    points, weights, interp, transfer, near_count, near_src, skel_group, skel_node, far_nodes
):
    g = lax.axis_index("leaf")
    x = lax.axis_index("help") // 2
    listed = jnp.where(lax.iota(jnp.int32, NEAR)[None, :] < near_count[0][:, None], near_src, -1)
    meta = jnp.pad(listed, ((0, 8 - OWN), (0, 128 - NEAR)), constant_values=-1)
    cloud, tgt, metas, far_out = spread(
        points, weights, interp, transfer, skel_group, skel_node, far_nodes, meta
    )
    slots = metas[:, :OWN, :NEAR].reshape(TGT, 1, NEAR)
    step = lax.iota(jnp.int32, SRC)
    ids = (g - 1 + step // 4) * 16 + x * 4 + step % 4
    ids = jnp.where(ids < 0, -2, ids)
    times = jnp.sum((slots == ids[None, :, None]).astype(jnp.int32), axis=2).reshape(-1)
    logs = jnp.log2(jnp.maximum(times, 1).astype(F32))
    part = near(times, logs, cloud, tgt)
    return fold(part, far_out)


def solution(mesh):
    placed = (
        P(None, ("leaf", "help")),
        P(None, ("leaf", "help")),
        P(("leaf", "help"), None, None),
        P(),
        P("leaf", "help"),
        P(("leaf", "help"), None),
        P("leaf", None),
        P(),
        P(),
    )
    return jax.shard_map(
        shards, mesh=mesh, in_specs=placed, out_specs=P(None, ("leaf", "help")), check_vma=False
    )
```

```python
import jax
import jax.numpy as jnp
from jax import lax
from jax.experimental import pallas as pl
from jax.experimental.pallas import tpu as pltpu
from jax.sharding import PartitionSpec as P

F = 64
R = 256
LEAF = 512
SK = 256
NEAR = 32
GROUPS = 16
HELP = 8
OWN = 2
COLS = OWN * LEAF
XS = 4
LEVELS = 4
UPPER = 14
STARTS = (0, 16, 24, 28)
NODES = 30
ROWS = R // HELP
PROWS = F // HELP
PARTS = 1 + R // F
ROOT = 0.8493218002880191
PEAK = 5.770780163555854

BF = jnp.bfloat16
F32 = jnp.float32
MESH = pl.DeviceIdType.MESH


def halves(value):
    high = value.astype(BF)
    return high, (value - high.astype(F32)).astype(BF)


def mul(left, right):
    return jnp.dot(left, right, preferred_element_type=F32)


def mul_t(left, right):
    return lax.dot_general(left, right, (((1,), (1,)), ((), ())), preferred_element_type=F32)


def product3(left, right, dot=mul):
    left_hi, left_lo = halves(left)
    right_hi, right_lo = halves(right)
    return dot(left_hi, right_hi) + dot(left_lo, right_hi) + dot(left_hi, right_lo)


def stacked_halves(pts):
    scaled = pts * ROOT
    high = scaled.astype(BF).astype(F32)
    low = (scaled - high).astype(BF).astype(F32)
    return jnp.concatenate([high, low], axis=0)


def target_side(both):
    high, low = both[:F], both[F:]
    whole = high + low
    own = PEAK - 0.5 * jnp.sum(whole * whole, axis=0, keepdims=True)
    high, low = high.astype(BF), low.astype(BF)
    return jnp.concatenate([high, high, low, low], axis=0), own


def source_side(both):
    turned = both.T
    whole = turned[:, :F] + turned[:, F:]
    own = PEAK - 0.5 * jnp.sum(whole * whole, axis=1, keepdims=True)
    turned = turned.astype(BF)
    return jnp.concatenate([turned, turned], axis=1), own


def remote(src, dst, send, recv, group, helper):
    return pltpu.make_async_remote_copy(
        src_ref=src,
        dst_ref=dst,
        send_sem=send,
        recv_sem=recv,
        device_id=(group, helper),
        device_id_type=MESH,
    )


def spread_kernel(
    pts, wts, interp, transfer, skg, skn, meta,
    cloud, tgt, metas, out_u, out_z,
    pts_v, wts_v, int_v, tr, skg_v, skn_v,
    ps_send, ps_buf, us_send, us_buf, lp_send, lp_buf, lu_send, p_buf, tier_u, tier_z,
    load_sem, y_send, y_recv, f_send, f_recv, s_send, s_recv, own_sem,
    t_send, t_recv, m_send, m_recv,
    ps_ss, ps_rs, us_ss, us_rs, lp_ss, lp_rs, lu_ss, lu_rs, p_ss, p_rs,
):
    g = lax.axis_index("leaf")
    h = lax.axis_index("help")
    x = lax.div(h, 2)
    core = lax.rem(h, 2)
    sib = h + 1 - 2 * core
    after = lax.rem(g + 1, GROUPS)
    before = lax.rem(g + GROUPS - 1, GROUPS)

    def helper_at(d):
        return lax.rem(h + d, HELP)

    def group_at(d):
        return lax.rem(g + d, GROUPS)

    barrier = pltpu.get_barrier_semaphore()

    @pl.loop(1, HELP)
    def _(d):
        pl.semaphore_signal(barrier, inc=1, device_id=(g, helper_at(d)), device_id_type=MESH)

    @pl.loop(1, GROUPS)
    def _(d):
        pl.semaphore_signal(barrier, inc=1, device_id=(group_at(d), h), device_id_type=MESH)

    pairs = (
        (pts, pts_v), (skg, skg_v), (wts, wts_v), (interp, int_v),
        (skn, skn_v), (transfer, tr),
    )
    loads = [
        pltpu.make_async_copy(src, dst, load_sem.at[i]) for i, (src, dst) in enumerate(pairs)
    ]
    for copy in loads:
        copy.start()

    def part(i):
        return pts if i == 0 else wts.at[pl.ds(F * (i - 1), F)]

    def y_copy(way, i):
        where = after if way == 0 else before
        return remote(
            part(i), cloud.at[2 * way, core, i], y_send.at[way, i], y_recv.at[way, i], where, h
        )

    def f_copy(way, i):
        spot = cloud.at[2 * way, core, i]
        return remote(spot, spot, f_send.at[way, i], f_recv.at[way, i], g, sib)

    sends = (g < GROUPS - 1, g > 0)

    def y_start(i):
        for way in range(2):
            pl.when(sends[way])(y_copy(way, i).start)

    def f_start(i):
        for way in range(2):

            @pl.when(sends[1 - way])
            def _(way=way):
                y_copy(way, i).wait_recv()
                f_copy(way, i).start()

    def s_copy(i):
        return remote(part(i), cloud.at[1, core, i], s_send.at[i], s_recv.at[i], g, sib)

    def own_copy(i):
        src = pts_v if i == 0 else wts_v.at[pl.ds(F * (i - 1), F)]
        return pltpu.make_async_copy(src, cloud.at[1, core, i], own_sem.at[i])

    def x_at(d):
        return lax.rem(x + d, XS) * 2 + core

    def t_copy(d):
        return remote(pts, tgt.at[x], t_send.at[d], t_recv.at[d], g, x_at(d))

    def m_copy(d):
        return remote(meta, metas.at[x], m_send.at[d], m_recv.at[d], g, x_at(d))

    own_t = pltpu.make_async_copy(pts_v, tgt.at[x], own_sem.at[PARTS])
    own_m = pltpu.make_async_copy(meta, metas.at[x], own_sem.at[PARTS + 1])

    loads[0].wait()
    loads[1].wait()
    picks = skg_v[...] - h * COLS
    onehot = (lax.broadcasted_iota(jnp.int32, (COLS, SK), 0) == picks).astype(BF)
    own_pts = pts_v[...]
    first = own_pts.astype(BF)
    rest = own_pts - first.astype(F32)
    second, third = halves(rest)
    chosen = mul(first, onehot) + mul(second, onehot) + mul(third, onehot)
    ps_send[...] = chosen.reshape(HELP, PROWS, SK)

    pl.semaphore_wait(barrier, HELP + GROUPS - 2)

    def ps_copy(d):
        to = helper_at(d)
        return remote(ps_send.at[to], ps_buf.at[h], ps_ss.at[d], ps_rs.at[d], g, to)

    def us_copy(d):
        to = helper_at(d)
        return remote(us_send.at[to], us_buf.at[h], us_ss.at[d], us_rs.at[d], g, to)

    def lp_copy(d):
        return remote(lp_send, lp_buf.at[g], lp_ss.at[d], lp_rs.at[d], group_at(d), h)

    def lu_copy(d):
        return remote(lu_send, tier_u.at[g], lu_ss.at[d], lu_rs.at[d], group_at(d), h)

    def p_copy(d):
        return remote(lp_buf, p_buf.at[h], p_ss.at[d], p_rs.at[d], g, helper_at(d))

    @pl.loop(1, HELP)
    def _(d):
        ps_copy(d).start()

    y_start(0)

    loads[2].wait()
    loads[3].wait()
    up = product3(wts_v[...], int_v[...].reshape(COLS, SK))
    us_send[...] = up.reshape(HELP, ROWS, SK)

    @pl.loop(1, HELP)
    def _(d):
        us_copy(d).start()

    y_start(1)

    @pl.loop(1, HELP)
    def _(d):
        ps_copy(d).wait_recv()

    ps_buf[h] = ps_send[h]
    total = ps_buf[0]
    for i in range(1, HELP):
        total = total + ps_buf[i]
    lp_send[...] = total
    lp_buf[g] = total

    @pl.loop(1, GROUPS)
    def _(d):
        lp_copy(d).start()

    @pl.loop(1, HELP)
    def _(d):
        us_copy(d).wait_recv()

    us_buf[h] = us_send[h]
    total = us_buf[0]
    for i in range(1, HELP):
        total = total + us_buf[i]
    lu_send[...] = total
    tier_u[g] = total

    @pl.loop(1, GROUPS)
    def _(d):
        lu_copy(d).start()

    y_start(2)
    y_start(3)

    @pl.loop(1, GROUPS)
    def _(d):
        lp_copy(d).wait_recv()

    @pl.loop(1, HELP)
    def _(d):
        p_copy(d).start()

    y_start(4)
    p_buf[h] = lp_buf[...]
    for d in range(1, XS):
        t_copy(d).start()
        m_copy(d).start()
    for i in range(PARTS):
        s_copy(i).start()
        own_copy(i).start()
    own_t.start()
    own_m.start()

    @pl.loop(1, GROUPS)
    def _(d):
        lu_copy(d).wait_recv()

    for copy in loads[4:]:
        copy.wait()

    @pl.loop(0, UPPER, unroll=2)
    def _(r):
        both = jnp.concatenate([tier_u[2 * r], tier_u[2 * r + 1]], axis=1)
        tier_u[GROUPS + r] = product3(both, tr[r])

    f_start(0)

    @pl.loop(1, HELP)
    def _(d):
        p_copy(d).wait_recv()

    @pl.loop(0, GROUPS)
    def _(n):
        tier_z[n] = stacked_halves(p_buf[:, n].reshape(F, SK)).astype(BF)

    rows = lax.broadcasted_iota(jnp.int32, (2 * SK, SK), 0)

    @pl.loop(0, UPPER, unroll=2)
    def _(r):
        both = jnp.concatenate([tier_z[2 * r], tier_z[2 * r + 1]], axis=1)
        pick = (rows == skn_v[pl.ds(r, 1), :]).astype(BF)
        tier_z[GROUPS + r] = mul(both, pick).astype(BF)

    tiers_out = (
        pltpu.make_async_copy(tier_u, out_u, own_sem.at[PARTS + 2]),
        pltpu.make_async_copy(tier_z, out_z, own_sem.at[PARTS + 3]),
    )
    for copy in tiers_out:
        copy.start()
    for i in range(1, PARTS):
        f_start(i)

    for i in range(PARTS):
        for way in range(2):
            pl.when(sends[1 - way])(f_copy(way, i).wait)
            pl.when(sends[way])(y_copy(way, i).wait_send)
        s_copy(i).wait()
        own_copy(i).wait()
    for d in range(1, XS):
        t_copy(d).wait()
        m_copy(d).wait()
    own_t.wait()
    own_m.wait()
    for copy in tiers_out:
        copy.wait()

    @pl.loop(1, HELP)
    def _(d):
        ps_copy(d).wait_send()
        us_copy(d).wait_send()
        p_copy(d).wait_send()

    @pl.loop(1, GROUPS)
    def _(d):
        lp_copy(d).wait_send()
        lu_copy(d).wait_send()


def spread(points, weights, interp, transfer, skel_group, skel_node, meta):
    anym = pl.BlockSpec(memory_space=pl.ANY)
    dma = pltpu.SemaphoreType.DMA
    return pl.pallas_call(
        spread_kernel,
        out_shape=(
            jax.ShapeDtypeStruct((3, 2, PARTS, F, COLS), F32),
            jax.ShapeDtypeStruct((XS, F, COLS), F32),
            jax.ShapeDtypeStruct((XS, OWN, NEAR), jnp.int32),
            jax.ShapeDtypeStruct((NODES, ROWS, SK), F32),
            jax.ShapeDtypeStruct((NODES, 2 * F, SK), BF),
        ),
        in_specs=[anym] * 7,
        out_specs=(anym,) * 5,
        scratch_shapes=[
            pltpu.VMEM((F, COLS), F32),
            pltpu.VMEM((R, COLS), F32),
            pltpu.VMEM((OWN, LEAF, SK), F32),
            pltpu.VMEM((UPPER, 2 * SK, SK), F32),
            pltpu.VMEM((1, SK), jnp.int32),
            pltpu.VMEM((UPPER, SK), jnp.int32),
            pltpu.VMEM((HELP, PROWS, SK), F32),
            pltpu.VMEM((HELP, PROWS, SK), F32),
            pltpu.VMEM((HELP, ROWS, SK), F32),
            pltpu.VMEM((HELP, ROWS, SK), F32),
            pltpu.VMEM((PROWS, SK), F32),
            pltpu.VMEM((GROUPS, PROWS, SK), F32),
            pltpu.VMEM((ROWS, SK), F32),
            pltpu.VMEM((HELP, GROUPS, PROWS, SK), F32),
            pltpu.VMEM((NODES, ROWS, SK), F32),
            pltpu.VMEM((NODES, 2 * F, SK), BF),
            dma((6,)),
            dma((2, PARTS)), dma((2, PARTS)),
            dma((2, PARTS)), dma((2, PARTS)),
            dma((PARTS,)), dma((PARTS,)),
            dma((PARTS + 4,)),
            dma((XS,)), dma((XS,)),
            dma((XS,)), dma((XS,)),
            dma((HELP,)), dma((HELP,)),
            dma((HELP,)), dma((HELP,)),
            dma((GROUPS,)), dma((GROUPS,)),
            dma((GROUPS,)), dma((GROUPS,)),
            dma((HELP,)), dma((HELP,)),
        ],
        compiler_params=pltpu.CompilerParams(
            collective_id=0, has_side_effects=True, vmem_limit_bytes=60 << 20
        ),
        name="spread",
    )(points, weights, interp, transfer, skel_group, skel_node, meta)


SRC = 3 * 2 * OWN
TGT = XS * OWN
CUT = 2


def near_kernel(
    times, logs, cloud, tgt, part,
    w_hl, left, source_own, right, target_own,
    list_t, list_s, list_log, hi_a, lo_a, hi_b, lo_b, cloud_v, tgt_v, sems,
):
    def cloud_copy(pair):
        step, core = lax.div(pair, 2), lax.rem(pair, 2)
        return pltpu.make_async_copy(cloud.at[step, core], cloud_v.at[pair], sems.at[pair])

    tgt_copy = pltpu.make_async_copy(tgt, tgt_v, sems.at[6])
    tgt_copy.start()
    for pair in range(6):
        cloud_copy(pair).start()
    tgt_copy.wait()
    @pl.loop(0, XS)
    def _(at):
        for j in range(OWN):
            factor, own = target_side(stacked_halves(tgt_v[at, :, j * LEAF:(j + 1) * LEAF]))
            right[at * OWN + j] = factor
            target_own[at * OWN + j] = jnp.broadcast_to(own, (8, LEAF))
            part[at * OWN + j] = jnp.zeros((R, LEAF), F32)

    @pl.loop(0, 6)
    def _(pair):
        cloud_copy(pair).wait()
        for j in range(OWN):
            span = slice(j * LEAF, (j + 1) * LEAF)
            s = pair * OWN + j
            for i in range(R // F):
                high, low = halves(cloud_v[pair, 1 + i, :, span])
                w_hl[s, i * F:(i + 1) * F, :] = high
                w_hl[s, R + i * F:R + (i + 1) * F, :] = low
            factor, own = source_side(stacked_halves(cloud_v[pair, 0, :, span]))
            left[s] = factor
            source_own[s] = jnp.broadcast_to(own, (LEAF, 128))

    def note(k, n):
        list_t[n] = lax.div(k, SRC)
        list_s[n] = lax.rem(k, SRC)
        list_log[n] = logs[k]
        return n + (times[k] > 0).astype(jnp.int32)

    count = lax.fori_loop(0, TGT * SRC, note, jnp.int32(0))
    for extra in range(2):
        list_t[count + extra] = 0
        list_s[count + extra] = 0
        list_log[count + extra] = jnp.float32(-1e30)

    def produce(i, hi, lo):
        t, s = list_t[i], list_s[i]
        shift = target_own[t, 0:1, :] + list_log[i]
        own = source_own[s]
        for c in range(CUT):
            n = LEAF // CUT
            span = slice(c * n, (c + 1) * n)
            cross = mul(left[s], right[t, :, span])
            block = jnp.exp2(cross + jnp.concatenate([own] * (n // 128), axis=1) + shift[:, span])
            high, low = halves(block)
            hi[:, span] = high
            lo[:, span] = low

    def consume(i, hi, lo):
        t, s = list_t[i], list_s[i]
        for c in range(CUT):
            n = LEAF // CUT
            span = slice(c * n, (c + 1) * n)
            two = mul(w_hl[s], hi[:, span])
            part[t, :, span] += two[:R] + two[R:] + mul(w_hl[s, :R], lo[:, span])

    produce(0, hi_a, lo_a)

    @pl.loop(0, lax.div(count + 1, 2))
    def _(k):
        produce(2 * k + 1, hi_b, lo_b)
        consume(2 * k, hi_a, lo_a)
        produce(jnp.minimum(2 * k + 2, count), hi_a, lo_a)
        consume(2 * k + 1, hi_b, lo_b)


def near(times, logs, cloud, tgt):
    vmem = pl.BlockSpec(memory_space=pltpu.VMEM)
    anym = pl.BlockSpec(memory_space=pl.ANY)
    smem = pl.BlockSpec(memory_space=pltpu.SMEM)
    return pl.pallas_call(
        near_kernel,
        out_shape=jax.ShapeDtypeStruct((TGT, R, LEAF), F32),
        in_specs=[smem, smem, anym, anym],
        out_specs=vmem,
        scratch_shapes=[
            pltpu.VMEM((SRC, 2 * R, LEAF), BF),
            pltpu.VMEM((SRC, LEAF, 4 * F), BF),
            pltpu.VMEM((SRC, LEAF, 128), F32),
            pltpu.VMEM((TGT, 4 * F, LEAF), BF),
            pltpu.VMEM((TGT, 8, LEAF), F32),
            pltpu.SMEM((TGT * SRC + 2,), jnp.int32),
            pltpu.SMEM((TGT * SRC + 2,), jnp.int32),
            pltpu.SMEM((TGT * SRC + 2,), F32),
            pltpu.VMEM((LEAF, LEAF), BF),
            pltpu.VMEM((LEAF, LEAF), BF),
            pltpu.VMEM((LEAF, LEAF), BF),
            pltpu.VMEM((LEAF, LEAF), BF),
            pltpu.VMEM((6, PARTS, F, COLS), F32),
            pltpu.VMEM((XS, F, COLS), F32),
            pltpu.SemaphoreType.DMA((7,)),
        ],
        compiler_params=pltpu.CompilerParams(vmem_limit_bytes=48 << 20),
        name="near",
    )(times, logs, cloud, tgt)


def fold_kernel(
    part, tier_u, tier_z, interp, transfer, far,
    out,
    first, last, u_v, z_v, int_v, half_v, far_s, v_buf,
    load_sem, first_ss, first_rs, last_ss, last_rs, v_ss, v_rs,
):
    g = lax.axis_index("leaf")
    h = lax.axis_index("help")
    x = lax.div(h, 2)
    core = lax.rem(h, 2)

    def helper_at(d):
        return lax.rem(h + d, HELP)

    def x_at(d):
        return lax.rem(x + d, XS)

    def beside(way):
        return x_at(1 if way == 0 else 3)

    def to(way):
        return beside(way) * 2 + core

    barrier = pltpu.get_barrier_semaphore()

    @pl.loop(1, HELP)
    def _(d):
        pl.semaphore_signal(barrier, inc=1, device_id=(g, helper_at(d)), device_id_type=MESH)

    pairs = [(far, far_s), (tier_z, z_v), (tier_u, u_v), (interp, int_v)]
    for level in range(1, LEVELS):
        r = STARTS[level] - GROUPS + lax.shift_right_logical(g, level)
        side = lax.rem(lax.shift_right_logical(g, level - 1), 2)
        rows = pl.ds(pl.multiple_of(side * SK, SK), SK)
        pairs.append((transfer.at[r, rows], half_v.at[level - 1]))
    loads = [
        pltpu.make_async_copy(src, dst, load_sem.at[i]) for i, (src, dst) in enumerate(pairs)
    ]
    for copy in loads:
        copy.start()
    pl.semaphore_wait(barrier, HELP - 1)

    def first_copy(way):
        src = part.at[x_at(2) * OWN + way]
        return remote(src, first.at[way], first_ss.at[way], first_rs.at[way], g, to(way))

    def plain_copy(way):
        src = part.at[beside(way) * OWN + 1 - way]
        dst = last.at[way, 1 - way]
        return remote(src, dst, last_ss.at[way, 0], last_rs.at[way, 0], g, to(way))

    def sum_copy(way):
        dst = last.at[way, way]
        return remote(first.at[way], dst, last_ss.at[way, 1], last_rs.at[way, 1], g, to(way))

    def v_copy(d):
        return remote(v_buf.at[h], v_buf.at[h], v_ss.at[d], v_rs.at[d], g, helper_at(d))

    for way in range(2):
        first_copy(way).start()
    for way in range(2):
        plain_copy(way).start()

    for copy in loads:
        copy.wait()
    sums = []
    for level in range(LEVELS):
        q = STARTS[level] + lax.shift_right_logical(g, level)
        right, target_own = target_side(z_v[q].astype(F32))
        nodes = [STARTS[level] + far_s[slot, q] for slot in range(4)]
        both = jnp.concatenate([z_v[node] for node in nodes], axis=1).astype(F32)
        left, source_own = source_side(both)
        block = jnp.exp2(mul(left, right) + source_own + target_own)
        values = jnp.concatenate([u_v[node] for node in nodes], axis=1)
        sums.append(product3(values, block))
    local = sums[LEVELS - 1]
    for level in range(LEVELS - 1, 0, -1):
        local = sums[level - 1] + product3(local, half_v[level - 1], mul_t)
    v_buf[h] = local

    @pl.loop(1, HELP)
    def _(d):
        v_copy(d).start()

    for way in range(2):
        first_copy(way).wait_recv()
        first[way] += part[beside(way) * OWN + way]
        sum_copy(way).start()

    @pl.loop(1, HELP)
    def _(d):
        v_copy(d).wait_recv()

    values = v_buf[...].reshape(R, SK)
    spans = [slice(j * LEAF, (j + 1) * LEAF) for j in range(OWN)]
    for j in range(OWN):
        out[:, spans[j]] = part[x * OWN + j] + product3(values, int_v[j], mul_t)
    for way in range(2):
        plain_copy(way).wait_recv()
        out[:, spans[1 - way]] += last[way, 1 - way]
    for way in range(2):
        sum_copy(way).wait_recv()
        out[:, spans[way]] += last[way, way]
    for way in range(2):
        first_copy(way).wait_send()
        plain_copy(way).wait_send()
        sum_copy(way).wait_send()

    @pl.loop(1, HELP)
    def _(d):
        v_copy(d).wait_send()


def fold(part, tier_u, tier_z, interp, transfer, far_slots):
    vmem = pl.BlockSpec(memory_space=pltpu.VMEM)
    anym = pl.BlockSpec(memory_space=pl.ANY)
    dma = pltpu.SemaphoreType.DMA
    return pl.pallas_call(
        fold_kernel,
        out_shape=jax.ShapeDtypeStruct((R, COLS), F32),
        in_specs=[vmem] + [anym] * 5,
        out_specs=vmem,
        scratch_shapes=[
            pltpu.VMEM((2, R, LEAF), F32),
            pltpu.VMEM((2, OWN, R, LEAF), F32),
            pltpu.VMEM((NODES, ROWS, SK), F32),
            pltpu.VMEM((NODES, 2 * F, SK), BF),
            pltpu.VMEM((OWN, LEAF, SK), F32),
            pltpu.VMEM((LEVELS - 1, SK, SK), F32),
            pltpu.SMEM((4, NODES), jnp.int32),
            pltpu.VMEM((HELP, ROWS, SK), F32),
            dma((7,)),
            dma((2,)), dma((2,)), dma((2, 2)), dma((2, 2)), dma((HELP,)), dma((HELP,)),
        ],
        compiler_params=pltpu.CompilerParams(
            collective_id=1, has_side_effects=True, vmem_limit_bytes=32 << 20
        ),
        name="fold",
    )(part, tier_u, tier_z, interp, transfer, far_slots)


def shards(
    points, weights, interp, transfer, near_count, near_src, skel_group, skel_node, far_nodes
):
    g = lax.axis_index("leaf")
    x = lax.axis_index("help") // 2
    listed = jnp.where(lax.iota(jnp.int32, NEAR)[None, :] < near_count[0][:, None], near_src, -1)
    cloud, tgt, metas, tier_u, tier_z = spread(
        points, weights, interp, transfer, skel_group, skel_node, listed
    )
    slots = metas.reshape(TGT, 1, NEAR)
    step = lax.iota(jnp.int32, SRC)
    ids = (g - 1 + step // 4) * 16 + x * 4 + step % 4
    ids = jnp.where(ids < 0, -2, ids)
    times = jnp.sum((slots == ids[None, :, None]).astype(jnp.int32), axis=2).reshape(-1)
    logs = jnp.log2(jnp.maximum(times, 1).astype(F32))
    part = near(times, logs, cloud, tgt)
    return fold(part, tier_u, tier_z, interp, transfer, far_nodes.T)


def solution(mesh):
    placed = (
        P(None, ("leaf", "help")),
        P(None, ("leaf", "help")),
        P(("leaf", "help"), None, None),
        P(),
        P("leaf", "help"),
        P(("leaf", "help"), None),
        P("leaf", None),
        P(),
        P(),
    )
    return jax.shard_map(
        shards, mesh=mesh, in_specs=placed, out_specs=P(None, ("leaf", "help")), check_vma=False
    )
```

```python
import jax
import jax.numpy as jnp
from jax import lax
from jax.experimental import pallas as pl
from jax.experimental.pallas import tpu as pltpu
from jax.sharding import PartitionSpec as P

F = 64
R = 256
LEAF = 512
SK = 256
NEAR = 32
GROUPS = 16
HELP = 8
OWN = 2
COLS = OWN * LEAF
XS = 4
LEVELS = 4
UPPER = 14
STARTS = (0, 16, 24, 28)
NODES = 30
ROWS = R // HELP
PROWS = F // HELP
PARTS = 1 + R // F
ROOT = 0.8493218002880191
PEAK = 5.770780163555854

BF = jnp.bfloat16
F32 = jnp.float32
MESH = pl.DeviceIdType.MESH


def halves(value):
    high = value.astype(BF)
    return high, (value - high.astype(F32)).astype(BF)


def mul(left, right):
    return jnp.dot(left, right, preferred_element_type=F32)


def mul_t(left, right):
    return lax.dot_general(left, right, (((1,), (1,)), ((), ())), preferred_element_type=F32)


def product3(left, right, dot=mul):
    left_hi, left_lo = halves(left)
    right_hi, right_lo = halves(right)
    return dot(left_hi, right_hi) + dot(left_lo, right_hi) + dot(left_hi, right_lo)


def stacked_halves(pts):
    scaled = pts * ROOT
    high = scaled.astype(BF).astype(F32)
    low = (scaled - high).astype(BF).astype(F32)
    return jnp.concatenate([high, low], axis=0)


def target_side(both):
    high, low = both[:F], both[F:]
    whole = high + low
    own = PEAK - 0.5 * jnp.sum(whole * whole, axis=0, keepdims=True)
    high, low = high.astype(BF), low.astype(BF)
    return jnp.concatenate([high, high, low, low], axis=0), own


def source_side(both):
    turned = both.T
    whole = turned[:, :F] + turned[:, F:]
    own = PEAK - 0.5 * jnp.sum(whole * whole, axis=1, keepdims=True)
    turned = turned.astype(BF)
    return jnp.concatenate([turned, turned], axis=1), own


def remote(src, dst, send, recv, group, helper):
    return pltpu.make_async_remote_copy(
        src_ref=src,
        dst_ref=dst,
        send_sem=send,
        recv_sem=recv,
        device_id=(group, helper),
        device_id_type=MESH,
    )


def spread_kernel(
    pts, wts, interp, transfer, skg, skn, far, meta,
    cloud, tgt, metas, own_v,
    pts_v, wts_v, int_v, tr, skg_v, skn_v, far_s,
    ps_send, ps_buf, us_send, us_buf, lp_send, lp_buf, lu_send, p_buf, tier_u, tier_z,
    load_sem, y_send, y_recv, f_send, f_recv, s_send, s_recv, own_sem,
    t_send, t_recv, m_send, m_recv,
    ps_ss, ps_rs, us_ss, us_rs, lp_ss, lp_rs, lu_ss, lu_rs, p_ss, p_rs,
):
    g = lax.axis_index("leaf")
    h = lax.axis_index("help")
    x = lax.div(h, 2)
    core = lax.rem(h, 2)
    sib = h + 1 - 2 * core
    after = lax.rem(g + 1, GROUPS)
    before = lax.rem(g + GROUPS - 1, GROUPS)

    def helper_at(d):
        return lax.rem(h + d, HELP)

    def group_at(d):
        return lax.rem(g + d, GROUPS)

    barrier = pltpu.get_barrier_semaphore()

    @pl.loop(1, HELP)
    def _(d):
        pl.semaphore_signal(barrier, inc=1, device_id=(g, helper_at(d)), device_id_type=MESH)

    @pl.loop(1, GROUPS)
    def _(d):
        pl.semaphore_signal(barrier, inc=1, device_id=(group_at(d), h), device_id_type=MESH)

    pairs = (
        (pts, pts_v), (skg, skg_v), (wts, wts_v), (interp, int_v),
        (skn, skn_v), (transfer, tr), (far, far_s),
    )
    loads = [
        pltpu.make_async_copy(src, dst, load_sem.at[i]) for i, (src, dst) in enumerate(pairs)
    ]
    for copy in loads:
        copy.start()

    def part(i):
        return pts if i == 0 else wts.at[pl.ds(F * (i - 1), F)]

    def y_copy(way, i):
        where = after if way == 0 else before
        return remote(
            part(i), cloud.at[2 * way, core, i], y_send.at[way, i], y_recv.at[way, i], where, h
        )

    def f_copy(way, i):
        spot = cloud.at[2 * way, core, i]
        return remote(spot, spot, f_send.at[way, i], f_recv.at[way, i], g, sib)

    sends = (g < GROUPS - 1, g > 0)

    def y_start(i):
        for way in range(2):
            pl.when(sends[way])(y_copy(way, i).start)

    def f_start(i):
        for way in range(2):

            @pl.when(sends[1 - way])
            def _(way=way):
                y_copy(way, i).wait_recv()
                f_copy(way, i).start()

    def s_copy(i):
        return remote(part(i), cloud.at[1, core, i], s_send.at[i], s_recv.at[i], g, sib)

    def own_copy(i):
        src = pts_v if i == 0 else wts_v.at[pl.ds(F * (i - 1), F)]
        return pltpu.make_async_copy(src, cloud.at[1, core, i], own_sem.at[i])

    def x_at(d):
        return lax.rem(x + d, XS) * 2 + core

    def t_copy(d):
        return remote(pts, tgt.at[x], t_send.at[d], t_recv.at[d], g, x_at(d))

    def m_copy(d):
        return remote(meta, metas.at[x], m_send.at[d], m_recv.at[d], g, x_at(d))

    own_t = pltpu.make_async_copy(pts_v, tgt.at[x], own_sem.at[PARTS])
    own_m = pltpu.make_async_copy(meta, metas.at[x], own_sem.at[PARTS + 1])

    loads[0].wait()
    loads[1].wait()
    picks = skg_v[...] - h * COLS
    onehot = (lax.broadcasted_iota(jnp.int32, (COLS, SK), 0) == picks).astype(BF)
    own_pts = pts_v[...]
    first = own_pts.astype(BF)
    rest = own_pts - first.astype(F32)
    second, third = halves(rest)
    chosen = mul(first, onehot) + mul(second, onehot) + mul(third, onehot)
    ps_send[...] = chosen.reshape(HELP, PROWS, SK)

    loads[2].wait()
    loads[3].wait()
    up = product3(wts_v[...], int_v[...].reshape(COLS, SK))
    us_send[...] = up.reshape(HELP, ROWS, SK)

    pl.semaphore_wait(barrier, HELP + GROUPS - 2)

    def ps_copy(d):
        to = helper_at(d)
        return remote(ps_send.at[to], ps_buf.at[h], ps_ss.at[d], ps_rs.at[d], g, to)

    def us_copy(d):
        to = helper_at(d)
        return remote(us_send.at[to], us_buf.at[h], us_ss.at[d], us_rs.at[d], g, to)

    def lp_copy(d):
        return remote(lp_send, lp_buf.at[g], lp_ss.at[d], lp_rs.at[d], group_at(d), h)

    def lu_copy(d):
        return remote(lu_send, tier_u.at[g], lu_ss.at[d], lu_rs.at[d], group_at(d), h)

    def p_copy(d):
        return remote(lp_buf, p_buf.at[h], p_ss.at[d], p_rs.at[d], g, helper_at(d))

    @pl.loop(1, HELP)
    def _(d):
        us_copy(d).start()
        ps_copy(d).start()

    y_start(0)
    @pl.loop(1, HELP)
    def _(d):
        us_copy(d).wait_recv()

    us_buf[h] = us_send[h]
    total = us_buf[0]
    for i in range(1, HELP):
        total = total + us_buf[i]
    lu_send[...] = total
    tier_u[g] = total

    @pl.loop(1, GROUPS)
    def _(d):
        lu_copy(d).start()

    @pl.loop(1, HELP)
    def _(d):
        ps_copy(d).wait_recv()

    ps_buf[h] = ps_send[h]
    total = ps_buf[0]
    for i in range(1, HELP):
        total = total + ps_buf[i]
    lp_send[...] = total
    lp_buf[g] = total

    @pl.loop(1, GROUPS)
    def _(d):
        lp_copy(d).start()

    y_start(1)
    y_start(2)

    @pl.loop(1, GROUPS)
    def _(d):
        lp_copy(d).wait_recv()

    @pl.loop(1, HELP)
    def _(d):
        p_copy(d).start()

    y_start(3)
    for d in range(1, XS):
        t_copy(d).start()
        m_copy(d).start()
    for i in range(PARTS):
        s_copy(i).start()
        own_copy(i).start()
    own_t.start()
    own_m.start()
    p_buf[h] = lp_buf[...]

    @pl.loop(1, GROUPS)
    def _(d):
        lu_copy(d).wait_recv()

    y_start(4)

    for copy in loads[4:]:
        copy.wait()

    @pl.loop(0, UPPER, unroll=2)
    def _(r):
        both = jnp.concatenate([tier_u[2 * r], tier_u[2 * r + 1]], axis=1)
        tier_u[GROUPS + r] = product3(both, tr[r])

    f_start(0)

    @pl.loop(1, HELP)
    def _(d):
        p_copy(d).wait_recv()

    @pl.loop(0, GROUPS)
    def _(n):
        tier_z[n] = stacked_halves(p_buf[:, n].reshape(F, SK)).astype(BF)

    rows = lax.broadcasted_iota(jnp.int32, (2 * SK, SK), 0)

    @pl.loop(0, UPPER, unroll=2)
    def _(r):
        both = jnp.concatenate([tier_z[2 * r], tier_z[2 * r + 1]], axis=1)
        pick = (rows == skn_v[pl.ds(r, 1), :]).astype(BF)
        tier_z[GROUPS + r] = mul(both, pick).astype(BF)

    f_start(1)
    sums = []
    for level in range(LEVELS):
        q = STARTS[level] + lax.shift_right_logical(g, level)
        right, target_own = target_side(tier_z[q].astype(F32))
        nodes = [STARTS[level] + far_s[slot, q] for slot in range(4)]
        both = jnp.concatenate([tier_z[node] for node in nodes], axis=1).astype(F32)
        left, source_own = source_side(both)
        block = jnp.exp2(mul(left, right) + source_own + target_own)
        values = jnp.concatenate([tier_u[node] for node in nodes], axis=1)
        sums.append(product3(values, block))
    f_start(2)
    local = sums[LEVELS - 1]
    for level in range(LEVELS - 1, 0, -1):
        r = STARTS[level] - GROUPS + lax.shift_right_logical(g, level)
        side = lax.rem(lax.shift_right_logical(g, level - 1), 2)
        half = tr[r, pl.ds(pl.multiple_of(side * SK, SK), SK), :]
        local = sums[level - 1] + product3(local, half, mul_t)
    own_v[...] = local
    for i in range(3, PARTS):
        f_start(i)

    for i in range(PARTS):
        for way in range(2):
            pl.when(sends[1 - way])(f_copy(way, i).wait)
            pl.when(sends[way])(y_copy(way, i).wait_send)
        s_copy(i).wait()
        own_copy(i).wait()
    for d in range(1, XS):
        t_copy(d).wait()
        m_copy(d).wait()
    own_t.wait()
    own_m.wait()

    @pl.loop(1, HELP)
    def _(d):
        ps_copy(d).wait_send()
        us_copy(d).wait_send()
        p_copy(d).wait_send()

    @pl.loop(1, GROUPS)
    def _(d):
        lp_copy(d).wait_send()
        lu_copy(d).wait_send()


def spread(points, weights, interp, transfer, skel_group, skel_node, far_slots, meta):
    vmem = pl.BlockSpec(memory_space=pltpu.VMEM)
    anym = pl.BlockSpec(memory_space=pl.ANY)
    dma = pltpu.SemaphoreType.DMA
    return pl.pallas_call(
        spread_kernel,
        out_shape=(
            jax.ShapeDtypeStruct((3, 2, PARTS, F, COLS), F32),
            jax.ShapeDtypeStruct((XS, F, COLS), F32),
            jax.ShapeDtypeStruct((XS, OWN, NEAR), jnp.int32),
            jax.ShapeDtypeStruct((ROWS, SK), F32),
        ),
        in_specs=[anym] * 8,
        out_specs=(anym, anym, anym, vmem),
        scratch_shapes=[
            pltpu.VMEM((F, COLS), F32),
            pltpu.VMEM((R, COLS), F32),
            pltpu.VMEM((OWN, LEAF, SK), F32),
            pltpu.VMEM((UPPER, 2 * SK, SK), F32),
            pltpu.VMEM((1, SK), jnp.int32),
            pltpu.VMEM((UPPER, SK), jnp.int32),
            pltpu.SMEM((4, NODES), jnp.int32),
            pltpu.VMEM((HELP, PROWS, SK), F32),
            pltpu.VMEM((HELP, PROWS, SK), F32),
            pltpu.VMEM((HELP, ROWS, SK), F32),
            pltpu.VMEM((HELP, ROWS, SK), F32),
            pltpu.VMEM((PROWS, SK), F32),
            pltpu.VMEM((GROUPS, PROWS, SK), F32),
            pltpu.VMEM((ROWS, SK), F32),
            pltpu.VMEM((HELP, GROUPS, PROWS, SK), F32),
            pltpu.VMEM((NODES, ROWS, SK), F32),
            pltpu.VMEM((NODES, 2 * F, SK), BF),
            dma((7,)),
            dma((2, PARTS)), dma((2, PARTS)),
            dma((2, PARTS)), dma((2, PARTS)),
            dma((PARTS,)), dma((PARTS,)),
            dma((PARTS + 2,)),
            dma((XS,)), dma((XS,)),
            dma((XS,)), dma((XS,)),
            dma((HELP,)), dma((HELP,)),
            dma((HELP,)), dma((HELP,)),
            dma((GROUPS,)), dma((GROUPS,)),
            dma((GROUPS,)), dma((GROUPS,)),
            dma((HELP,)), dma((HELP,)),
        ],
        compiler_params=pltpu.CompilerParams(
            collective_id=0, has_side_effects=True, vmem_limit_bytes=60 << 20
        ),
        name="spread",
    )(points, weights, interp, transfer, skel_group, skel_node, far_slots, meta)


SRC = 3 * 2 * OWN
TGT = XS * OWN
CUT = 2


def near_kernel(
    times, logs, cloud, tgt, part,
    w_hl, left, source_own, right, target_own,
    list_t, list_s, list_log, hi_a, lo_a, hi_b, lo_b, cloud_v, tgt_v, sems,
):
    def cloud_copy(pair):
        step, core = lax.div(pair, 2), lax.rem(pair, 2)
        return pltpu.make_async_copy(cloud.at[step, core], cloud_v.at[pair], sems.at[pair])

    tgt_copy = pltpu.make_async_copy(tgt, tgt_v, sems.at[6])
    tgt_copy.start()
    for pair in range(6):
        cloud_copy(pair).start()
    tgt_copy.wait()
    @pl.loop(0, XS)
    def _(at):
        for j in range(OWN):
            factor, own = target_side(stacked_halves(tgt_v[at, :, j * LEAF:(j + 1) * LEAF]))
            right[at * OWN + j] = factor
            target_own[at * OWN + j] = jnp.broadcast_to(own, (8, LEAF))
            part[at * OWN + j] = jnp.zeros((R, LEAF), F32)

    @pl.loop(0, 6)
    def _(pair):
        cloud_copy(pair).wait()
        for j in range(OWN):
            span = slice(j * LEAF, (j + 1) * LEAF)
            s = pair * OWN + j
            for i in range(R // F):
                high, low = halves(cloud_v[pair, 1 + i, :, span])
                w_hl[s, i * F:(i + 1) * F, :] = high
                w_hl[s, R + i * F:R + (i + 1) * F, :] = low
            factor, own = source_side(stacked_halves(cloud_v[pair, 0, :, span]))
            left[s] = factor
            source_own[s] = jnp.broadcast_to(own, (LEAF, 128))

    def note(k, n):
        list_t[n] = lax.div(k, SRC)
        list_s[n] = lax.rem(k, SRC)
        list_log[n] = logs[k]
        return n + (times[k] > 0).astype(jnp.int32)

    count = lax.fori_loop(0, TGT * SRC, note, jnp.int32(0))
    for extra in range(2):
        list_t[count + extra] = 0
        list_s[count + extra] = 0
        list_log[count + extra] = jnp.float32(-1e30)

    def produce(i, hi, lo):
        t, s = list_t[i], list_s[i]
        shift = target_own[t, 0:1, :] + list_log[i]
        own = source_own[s]
        for c in range(CUT):
            n = LEAF // CUT
            span = slice(c * n, (c + 1) * n)
            cross = mul(left[s], right[t, :, span])
            block = jnp.exp2(cross + jnp.concatenate([own] * (n // 128), axis=1) + shift[:, span])
            high, low = halves(block)
            hi[:, span] = high
            lo[:, span] = low

    def consume(i, hi, lo):
        t, s = list_t[i], list_s[i]
        for c in range(CUT):
            n = LEAF // CUT
            span = slice(c * n, (c + 1) * n)
            two = mul(w_hl[s], hi[:, span])
            part[t, :, span] += two[:R] + two[R:] + mul(w_hl[s, :R], lo[:, span])

    produce(0, hi_a, lo_a)

    @pl.loop(0, lax.div(count + 1, 2))
    def _(k):
        produce(2 * k + 1, hi_b, lo_b)
        consume(2 * k, hi_a, lo_a)
        produce(jnp.minimum(2 * k + 2, count), hi_a, lo_a)
        consume(2 * k + 1, hi_b, lo_b)


def near(times, logs, cloud, tgt):
    vmem = pl.BlockSpec(memory_space=pltpu.VMEM)
    anym = pl.BlockSpec(memory_space=pl.ANY)
    smem = pl.BlockSpec(memory_space=pltpu.SMEM)
    return pl.pallas_call(
        near_kernel,
        out_shape=jax.ShapeDtypeStruct((TGT, R, LEAF), F32),
        in_specs=[smem, smem, anym, anym],
        out_specs=vmem,
        scratch_shapes=[
            pltpu.VMEM((SRC, 2 * R, LEAF), BF),
            pltpu.VMEM((SRC, LEAF, 4 * F), BF),
            pltpu.VMEM((SRC, LEAF, 128), F32),
            pltpu.VMEM((TGT, 4 * F, LEAF), BF),
            pltpu.VMEM((TGT, 8, LEAF), F32),
            pltpu.SMEM((TGT * SRC + 2,), jnp.int32),
            pltpu.SMEM((TGT * SRC + 2,), jnp.int32),
            pltpu.SMEM((TGT * SRC + 2,), F32),
            pltpu.VMEM((LEAF, LEAF), BF),
            pltpu.VMEM((LEAF, LEAF), BF),
            pltpu.VMEM((LEAF, LEAF), BF),
            pltpu.VMEM((LEAF, LEAF), BF),
            pltpu.VMEM((6, PARTS, F, COLS), F32),
            pltpu.VMEM((XS, F, COLS), F32),
            pltpu.SemaphoreType.DMA((7,)),
        ],
        compiler_params=pltpu.CompilerParams(vmem_limit_bytes=48 << 20),
        name="near",
    )(times, logs, cloud, tgt)


def fold_kernel(
    part, own_v, interp,
    out,
    first, last, int_v, v_buf,
    load_sem, first_ss, first_rs, last_ss, last_rs, v_ss, v_rs,
):
    g = lax.axis_index("leaf")
    h = lax.axis_index("help")
    x = lax.div(h, 2)
    core = lax.rem(h, 2)

    def helper_at(d):
        return lax.rem(h + d, HELP)

    def x_at(d):
        return lax.rem(x + d, XS)

    def beside(way):
        return x_at(1 if way == 0 else 3)

    def to(way):
        return beside(way) * 2 + core

    barrier = pltpu.get_barrier_semaphore()

    @pl.loop(1, HELP)
    def _(d):
        pl.semaphore_signal(barrier, inc=1, device_id=(g, helper_at(d)), device_id_type=MESH)

    load = pltpu.make_async_copy(interp, int_v, load_sem)
    load.start()
    pl.semaphore_wait(barrier, HELP - 1)

    def first_copy(way):
        src = part.at[x_at(2) * OWN + way]
        return remote(src, first.at[way], first_ss.at[way], first_rs.at[way], g, to(way))

    def plain_copy(way):
        src = part.at[beside(way) * OWN + 1 - way]
        dst = last.at[way, 1 - way]
        return remote(src, dst, last_ss.at[way, 0], last_rs.at[way, 0], g, to(way))

    def sum_copy(way):
        dst = last.at[way, way]
        return remote(first.at[way], dst, last_ss.at[way, 1], last_rs.at[way, 1], g, to(way))

    def v_copy(d):
        return remote(own_v, v_buf.at[h], v_ss.at[d], v_rs.at[d], g, helper_at(d))

    @pl.loop(1, HELP)
    def _(d):
        v_copy(d).start()

    for way in range(2):
        first_copy(way).start()
    for way in range(2):
        plain_copy(way).start()
    v_buf[h] = own_v[...]
    load.wait()

    for way in range(2):
        first_copy(way).wait_recv()
        first[way] += part[beside(way) * OWN + way]
        sum_copy(way).start()

    @pl.loop(1, HELP)
    def _(d):
        v_copy(d).wait_recv()

    values = v_buf[...].reshape(R, SK)
    spans = [slice(j * LEAF, (j + 1) * LEAF) for j in range(OWN)]
    for j in range(OWN):
        out[:, spans[j]] = part[x * OWN + j] + product3(values, int_v[j], mul_t)
    for way in range(2):
        plain_copy(way).wait_recv()
        out[:, spans[1 - way]] += last[way, 1 - way]
    for way in range(2):
        sum_copy(way).wait_recv()
        out[:, spans[way]] += last[way, way]
    for way in range(2):
        first_copy(way).wait_send()
        plain_copy(way).wait_send()
        sum_copy(way).wait_send()

    @pl.loop(1, HELP)
    def _(d):
        v_copy(d).wait_send()


def fold(part, own_v, interp):
    vmem = pl.BlockSpec(memory_space=pltpu.VMEM)
    anym = pl.BlockSpec(memory_space=pl.ANY)
    dma = pltpu.SemaphoreType.DMA
    return pl.pallas_call(
        fold_kernel,
        out_shape=jax.ShapeDtypeStruct((R, COLS), F32),
        in_specs=[vmem, vmem, anym],
        out_specs=vmem,
        scratch_shapes=[
            pltpu.VMEM((2, R, LEAF), F32),
            pltpu.VMEM((2, OWN, R, LEAF), F32),
            pltpu.VMEM((OWN, LEAF, SK), F32),
            pltpu.VMEM((HELP, ROWS, SK), F32),
            dma,
            dma((2,)), dma((2,)), dma((2, 2)), dma((2, 2)), dma((HELP,)), dma((HELP,)),
        ],
        compiler_params=pltpu.CompilerParams(
            collective_id=1, has_side_effects=True, vmem_limit_bytes=32 << 20
        ),
        name="fold",
    )(part, own_v, interp)


def shards(
    points, weights, interp, transfer, near_count, near_src, skel_group, skel_node, far_nodes
):
    g = lax.axis_index("leaf")
    x = lax.axis_index("help") // 2
    listed = jnp.where(lax.iota(jnp.int32, NEAR)[None, :] < near_count[0][:, None], near_src, -1)
    cloud, tgt, metas, own_v = spread(
        points, weights, interp, transfer, skel_group, skel_node, far_nodes.T, listed
    )
    slots = metas.reshape(TGT, 1, NEAR)
    step = lax.iota(jnp.int32, SRC)
    ids = (g - 1 + step // 4) * 16 + x * 4 + step % 4
    ids = jnp.where(ids < 0, -2, ids)
    times = jnp.sum((slots == ids[None, :, None]).astype(jnp.int32), axis=2).reshape(-1)
    logs = jnp.log2(jnp.maximum(times, 1).astype(F32))
    part = near(times, logs, cloud, tgt)
    return fold(part, own_v, interp)


def solution(mesh):
    placed = (
        P(None, ("leaf", "help")),
        P(None, ("leaf", "help")),
        P(("leaf", "help"), None, None),
        P(),
        P("leaf", "help"),
        P(("leaf", "help"), None),
        P("leaf", None),
        P(),
        P(),
    )
    return jax.shard_map(
        shards, mesh=mesh, in_specs=placed, out_specs=P(None, ("leaf", "help")), check_vma=False
    )
```

```python
import jax
import jax.numpy as jnp
from jax import lax
from jax.experimental import pallas as pl
from jax.experimental.pallas import tpu as pltpu
from jax.sharding import PartitionSpec as P

F = 64
R = 256
LEAF = 512
SK = 256
NEAR = 32
GROUPS = 16
HELP = 8
OWN = 2
COLS = OWN * LEAF
XS = 4
LEVELS = 4
UPPER = 14
STARTS = (0, 16, 24, 28)
NODES = 30
ROWS = R // HELP
PROWS = F // HELP
PARTS = 1 + R // F
ROOT = 0.8493218002880191
PEAK = 5.770780163555854

BF = jnp.bfloat16
F32 = jnp.float32
MESH = pl.DeviceIdType.MESH


def halves(value):
    high = value.astype(BF)
    return high, (value - high.astype(F32)).astype(BF)


def mul(left, right):
    return jnp.dot(left, right, preferred_element_type=F32)


def mul_t(left, right):
    return lax.dot_general(left, right, (((1,), (1,)), ((), ())), preferred_element_type=F32)


def product3(left, right, dot=mul):
    left_hi, left_lo = halves(left)
    right_hi, right_lo = halves(right)
    return dot(left_hi, right_hi) + dot(left_lo, right_hi) + dot(left_hi, right_lo)


def stacked_halves(pts):
    scaled = pts * ROOT
    high = scaled.astype(BF).astype(F32)
    low = (scaled - high).astype(BF).astype(F32)
    return jnp.concatenate([high, low], axis=0)


def target_side(both):
    high, low = both[:F], both[F:]
    whole = high + low
    own = PEAK - 0.5 * jnp.sum(whole * whole, axis=0, keepdims=True)
    high, low = high.astype(BF), low.astype(BF)
    return jnp.concatenate([high, high, low, low], axis=0), own


def source_side(both):
    turned = both.T
    whole = turned[:, :F] + turned[:, F:]
    own = PEAK - 0.5 * jnp.sum(whole * whole, axis=1, keepdims=True)
    turned = turned.astype(BF)
    return jnp.concatenate([turned, turned], axis=1), own


def remote(src, dst, send, recv, group, helper):
    return pltpu.make_async_remote_copy(
        src_ref=src,
        dst_ref=dst,
        send_sem=send,
        recv_sem=recv,
        device_id=(group, helper),
        device_id_type=MESH,
    )


def spread_kernel(
    pts, wts, interp, transfer, skg, skn, far, meta,
    cloud, tgt, metas, v_out,
    pts_v, wts_v, int_v, tr, skg_v, skn_v, far_s,
    ps_send, ps_buf, us_send, us_buf, lp_send, lp_buf, lu_send, p_buf, tier_u, tier_z, v_buf,
    load_sem, y_send, y_recv, f_send, f_recv, s_send, s_recv, own_sem,
    t_send, t_recv, m_send, m_recv,
    ps_ss, ps_rs, us_ss, us_rs, lp_ss, lp_rs, lu_ss, lu_rs, p_ss, p_rs, v_ss, v_rs,
):
    g = lax.axis_index("leaf")
    h = lax.axis_index("help")
    x = lax.div(h, 2)
    core = lax.rem(h, 2)
    sib = h + 1 - 2 * core
    after = lax.rem(g + 1, GROUPS)
    before = lax.rem(g + GROUPS - 1, GROUPS)

    def helper_at(d):
        return lax.rem(h + d, HELP)

    def group_at(d):
        return lax.rem(g + d, GROUPS)

    barrier = pltpu.get_barrier_semaphore()

    @pl.loop(1, HELP)
    def _(d):
        pl.semaphore_signal(barrier, inc=1, device_id=(g, helper_at(d)), device_id_type=MESH)

    @pl.loop(1, GROUPS)
    def _(d):
        pl.semaphore_signal(barrier, inc=1, device_id=(group_at(d), h), device_id_type=MESH)

    pairs = (
        (pts, pts_v), (skg, skg_v), (wts, wts_v), (interp, int_v),
        (skn, skn_v), (transfer, tr), (far, far_s),
    )
    loads = [
        pltpu.make_async_copy(src, dst, load_sem.at[i]) for i, (src, dst) in enumerate(pairs)
    ]
    for copy in loads:
        copy.start()

    def part(i):
        return pts if i == 0 else wts.at[pl.ds(F * (i - 1), F)]

    def y_copy(way, i):
        where = after if way == 0 else before
        return remote(
            part(i), cloud.at[2 * way, core, i], y_send.at[way, i], y_recv.at[way, i], where, h
        )

    def f_copy(way, i):
        spot = cloud.at[2 * way, core, i]
        return remote(spot, spot, f_send.at[way, i], f_recv.at[way, i], g, sib)

    sends = (g < GROUPS - 1, g > 0)

    def y_start(i):
        for way in range(2):
            pl.when(sends[way])(y_copy(way, i).start)

    def f_start(i):
        for way in range(2):

            @pl.when(sends[1 - way])
            def _(way=way):
                y_copy(way, i).wait_recv()
                f_copy(way, i).start()

    def s_copy(i):
        return remote(part(i), cloud.at[1, core, i], s_send.at[i], s_recv.at[i], g, sib)

    def own_copy(i):
        src = pts_v if i == 0 else wts_v.at[pl.ds(F * (i - 1), F)]
        return pltpu.make_async_copy(src, cloud.at[1, core, i], own_sem.at[i])

    def x_at(d):
        return lax.rem(x + d, XS) * 2 + core

    def t_copy(d):
        return remote(pts, tgt.at[x], t_send.at[d], t_recv.at[d], g, x_at(d))

    def m_copy(d):
        return remote(meta, metas.at[x], m_send.at[d], m_recv.at[d], g, x_at(d))

    own_t = pltpu.make_async_copy(pts_v, tgt.at[x], own_sem.at[PARTS])
    own_m = pltpu.make_async_copy(meta, metas.at[x], own_sem.at[PARTS + 1])

    loads[0].wait()
    loads[1].wait()
    picks = skg_v[...] - h * COLS
    onehot = (lax.broadcasted_iota(jnp.int32, (COLS, SK), 0) == picks).astype(BF)
    own_pts = pts_v[...]
    first = own_pts.astype(BF)
    rest = own_pts - first.astype(F32)
    second, third = halves(rest)
    chosen = mul(first, onehot) + mul(second, onehot) + mul(third, onehot)
    ps_send[...] = chosen.reshape(HELP, PROWS, SK)

    loads[2].wait()
    loads[3].wait()
    up = product3(wts_v[...], int_v[...].reshape(COLS, SK))
    us_send[...] = up.reshape(HELP, ROWS, SK)

    pl.semaphore_wait(barrier, HELP + GROUPS - 2)

    def ps_copy(d):
        to = helper_at(d)
        return remote(ps_send.at[to], ps_buf.at[h], ps_ss.at[d], ps_rs.at[d], g, to)

    def us_copy(d):
        to = helper_at(d)
        return remote(us_send.at[to], us_buf.at[h], us_ss.at[d], us_rs.at[d], g, to)

    def lp_copy(d):
        return remote(lp_send, lp_buf.at[g], lp_ss.at[d], lp_rs.at[d], group_at(d), h)

    def lu_copy(d):
        return remote(lu_send, tier_u.at[g], lu_ss.at[d], lu_rs.at[d], group_at(d), h)

    def p_copy(d):
        return remote(lp_buf, p_buf.at[h], p_ss.at[d], p_rs.at[d], g, helper_at(d))

    def v_copy(d):
        return remote(v_buf.at[h], v_buf.at[h], v_ss.at[d], v_rs.at[d], g, helper_at(d))

    @pl.loop(1, HELP)
    def _(d):
        us_copy(d).start()
        ps_copy(d).start()

    y_start(0)
    @pl.loop(1, HELP)
    def _(d):
        us_copy(d).wait_recv()

    us_buf[h] = us_send[h]
    total = us_buf[0]
    for i in range(1, HELP):
        total = total + us_buf[i]
    lu_send[...] = total
    tier_u[g] = total

    @pl.loop(1, GROUPS)
    def _(d):
        lu_copy(d).start()

    @pl.loop(1, HELP)
    def _(d):
        ps_copy(d).wait_recv()

    ps_buf[h] = ps_send[h]
    total = ps_buf[0]
    for i in range(1, HELP):
        total = total + ps_buf[i]
    lp_send[...] = total
    lp_buf[g] = total

    @pl.loop(1, GROUPS)
    def _(d):
        lp_copy(d).start()

    y_start(1)
    y_start(2)

    @pl.loop(1, GROUPS)
    def _(d):
        lp_copy(d).wait_recv()

    @pl.loop(1, HELP)
    def _(d):
        p_copy(d).start()

    y_start(3)
    for d in range(1, XS):
        t_copy(d).start()
        m_copy(d).start()
    for i in range(PARTS):
        s_copy(i).start()
        own_copy(i).start()
    own_t.start()
    own_m.start()
    p_buf[h] = lp_buf[...]

    @pl.loop(1, GROUPS)
    def _(d):
        lu_copy(d).wait_recv()

    y_start(4)

    for copy in loads[4:]:
        copy.wait()

    @pl.loop(0, UPPER, unroll=2)
    def _(r):
        both = jnp.concatenate([tier_u[2 * r], tier_u[2 * r + 1]], axis=1)
        tier_u[GROUPS + r] = product3(both, tr[r])

    f_start(0)

    @pl.loop(1, HELP)
    def _(d):
        p_copy(d).wait_recv()

    @pl.loop(0, GROUPS)
    def _(n):
        tier_z[n] = stacked_halves(p_buf[:, n].reshape(F, SK)).astype(BF)

    rows = lax.broadcasted_iota(jnp.int32, (2 * SK, SK), 0)

    @pl.loop(0, UPPER, unroll=2)
    def _(r):
        both = jnp.concatenate([tier_z[2 * r], tier_z[2 * r + 1]], axis=1)
        pick = (rows == skn_v[pl.ds(r, 1), :]).astype(BF)
        tier_z[GROUPS + r] = mul(both, pick).astype(BF)

    f_start(1)
    sums = []
    for level in range(LEVELS):
        q = STARTS[level] + lax.shift_right_logical(g, level)
        right, target_own = target_side(tier_z[q].astype(F32))
        nodes = [STARTS[level] + far_s[slot, q] for slot in range(4)]
        both = jnp.concatenate([tier_z[node] for node in nodes], axis=1).astype(F32)
        left, source_own = source_side(both)
        block = jnp.exp2(mul(left, right) + source_own + target_own)
        values = jnp.concatenate([tier_u[node] for node in nodes], axis=1)
        sums.append(product3(values, block))
    f_start(2)
    local = sums[LEVELS - 1]
    for level in range(LEVELS - 1, 0, -1):
        r = STARTS[level] - GROUPS + lax.shift_right_logical(g, level)
        side = lax.rem(lax.shift_right_logical(g, level - 1), 2)
        half = tr[r, pl.ds(pl.multiple_of(side * SK, SK), SK), :]
        local = sums[level - 1] + product3(local, half, mul_t)
    v_buf[h] = local

    @pl.loop(1, HELP)
    def _(d):
        v_copy(d).start()

    for i in range(3, PARTS):
        f_start(i)

    @pl.loop(1, HELP)
    def _(d):
        v_copy(d).wait_recv()

    v_out[...] = v_buf[...].reshape(R, SK)

    for i in range(PARTS):
        for way in range(2):
            pl.when(sends[1 - way])(f_copy(way, i).wait)
            pl.when(sends[way])(y_copy(way, i).wait_send)
        s_copy(i).wait()
        own_copy(i).wait()
    for d in range(1, XS):
        t_copy(d).wait()
        m_copy(d).wait()
    own_t.wait()
    own_m.wait()

    @pl.loop(1, HELP)
    def _(d):
        ps_copy(d).wait_send()
        us_copy(d).wait_send()
        p_copy(d).wait_send()
        v_copy(d).wait_send()

    @pl.loop(1, GROUPS)
    def _(d):
        lp_copy(d).wait_send()
        lu_copy(d).wait_send()


def spread(points, weights, interp, transfer, skel_group, skel_node, far_slots, meta):
    vmem = pl.BlockSpec(memory_space=pltpu.VMEM)
    anym = pl.BlockSpec(memory_space=pl.ANY)
    dma = pltpu.SemaphoreType.DMA
    return pl.pallas_call(
        spread_kernel,
        out_shape=(
            jax.ShapeDtypeStruct((3, 2, PARTS, F, COLS), F32),
            jax.ShapeDtypeStruct((XS, F, COLS), F32),
            jax.ShapeDtypeStruct((XS, OWN, NEAR), jnp.int32),
            jax.ShapeDtypeStruct((R, SK), F32),
        ),
        in_specs=[anym] * 8,
        out_specs=(anym, anym, anym, vmem),
        scratch_shapes=[
            pltpu.VMEM((F, COLS), F32),
            pltpu.VMEM((R, COLS), F32),
            pltpu.VMEM((OWN, LEAF, SK), F32),
            pltpu.VMEM((UPPER, 2 * SK, SK), F32),
            pltpu.VMEM((1, SK), jnp.int32),
            pltpu.VMEM((UPPER, SK), jnp.int32),
            pltpu.SMEM((4, NODES), jnp.int32),
            pltpu.VMEM((HELP, PROWS, SK), F32),
            pltpu.VMEM((HELP, PROWS, SK), F32),
            pltpu.VMEM((HELP, ROWS, SK), F32),
            pltpu.VMEM((HELP, ROWS, SK), F32),
            pltpu.VMEM((PROWS, SK), F32),
            pltpu.VMEM((GROUPS, PROWS, SK), F32),
            pltpu.VMEM((ROWS, SK), F32),
            pltpu.VMEM((HELP, GROUPS, PROWS, SK), F32),
            pltpu.VMEM((NODES, ROWS, SK), F32),
            pltpu.VMEM((NODES, 2 * F, SK), BF),
            pltpu.VMEM((HELP, ROWS, SK), F32),
            dma((7,)),
            dma((2, PARTS)), dma((2, PARTS)),
            dma((2, PARTS)), dma((2, PARTS)),
            dma((PARTS,)), dma((PARTS,)),
            dma((PARTS + 2,)),
            dma((XS,)), dma((XS,)),
            dma((XS,)), dma((XS,)),
            dma((HELP,)), dma((HELP,)),
            dma((HELP,)), dma((HELP,)),
            dma((GROUPS,)), dma((GROUPS,)),
            dma((GROUPS,)), dma((GROUPS,)),
            dma((HELP,)), dma((HELP,)),
            dma((HELP,)), dma((HELP,)),
        ],
        compiler_params=pltpu.CompilerParams(
            collective_id=0, has_side_effects=True, vmem_limit_bytes=60 << 20
        ),
        name="spread",
    )(points, weights, interp, transfer, skel_group, skel_node, far_slots, meta)


SRC = 3 * 2 * OWN
TGT = XS * OWN
CUT = 2


def near_kernel(
    times, logs, cloud, tgt, part,
    w_hl, left, source_own, right, target_own,
    list_t, list_s, list_log, hi_a, lo_a, hi_b, lo_b, cloud_v, tgt_v, sems,
):
    def cloud_copy(pair):
        step, core = lax.div(pair, 2), lax.rem(pair, 2)
        return pltpu.make_async_copy(cloud.at[step, core], cloud_v.at[pair], sems.at[pair])

    tgt_copy = pltpu.make_async_copy(tgt, tgt_v, sems.at[6])
    tgt_copy.start()
    for pair in range(6):
        cloud_copy(pair).start()
    tgt_copy.wait()
    @pl.loop(0, XS)
    def _(at):
        for j in range(OWN):
            factor, own = target_side(stacked_halves(tgt_v[at, :, j * LEAF:(j + 1) * LEAF]))
            right[at * OWN + j] = factor
            target_own[at * OWN + j] = jnp.broadcast_to(own, (8, LEAF))
            part[at * OWN + j] = jnp.zeros((R, LEAF), F32)

    @pl.loop(0, 6)
    def _(pair):
        cloud_copy(pair).wait()
        for j in range(OWN):
            span = slice(j * LEAF, (j + 1) * LEAF)
            s = pair * OWN + j
            for i in range(R // F):
                high, low = halves(cloud_v[pair, 1 + i, :, span])
                w_hl[s, i * F:(i + 1) * F, :] = high
                w_hl[s, R + i * F:R + (i + 1) * F, :] = low
            factor, own = source_side(stacked_halves(cloud_v[pair, 0, :, span]))
            left[s] = factor
            source_own[s] = jnp.broadcast_to(own, (LEAF, 128))

    def note(k, n):
        list_t[n] = lax.div(k, SRC)
        list_s[n] = lax.rem(k, SRC)
        list_log[n] = logs[k]
        return n + (times[k] > 0).astype(jnp.int32)

    count = lax.fori_loop(0, TGT * SRC, note, jnp.int32(0))
    for extra in range(2):
        list_t[count + extra] = 0
        list_s[count + extra] = 0
        list_log[count + extra] = jnp.float32(-1e30)

    def produce(i, hi, lo):
        t, s = list_t[i], list_s[i]
        shift = target_own[t, 0:1, :] + list_log[i]
        own = source_own[s]
        for c in range(CUT):
            n = LEAF // CUT
            span = slice(c * n, (c + 1) * n)
            cross = mul(left[s], right[t, :, span])
            block = jnp.exp2(cross + jnp.concatenate([own] * (n // 128), axis=1) + shift[:, span])
            high, low = halves(block)
            hi[:, span] = high
            lo[:, span] = low

    def consume(i, hi, lo):
        t, s = list_t[i], list_s[i]
        for c in range(CUT):
            n = LEAF // CUT
            span = slice(c * n, (c + 1) * n)
            two = mul(w_hl[s], hi[:, span])
            part[t, :, span] += two[:R] + two[R:] + mul(w_hl[s, :R], lo[:, span])

    produce(0, hi_a, lo_a)

    @pl.loop(0, lax.div(count + 1, 2))
    def _(k):
        produce(2 * k + 1, hi_b, lo_b)
        consume(2 * k, hi_a, lo_a)
        produce(jnp.minimum(2 * k + 2, count), hi_a, lo_a)
        consume(2 * k + 1, hi_b, lo_b)


def near(times, logs, cloud, tgt):
    vmem = pl.BlockSpec(memory_space=pltpu.VMEM)
    anym = pl.BlockSpec(memory_space=pl.ANY)
    smem = pl.BlockSpec(memory_space=pltpu.SMEM)
    return pl.pallas_call(
        near_kernel,
        out_shape=jax.ShapeDtypeStruct((TGT, R, LEAF), F32),
        in_specs=[smem, smem, anym, anym],
        out_specs=vmem,
        scratch_shapes=[
            pltpu.VMEM((SRC, 2 * R, LEAF), BF),
            pltpu.VMEM((SRC, LEAF, 4 * F), BF),
            pltpu.VMEM((SRC, LEAF, 128), F32),
            pltpu.VMEM((TGT, 4 * F, LEAF), BF),
            pltpu.VMEM((TGT, 8, LEAF), F32),
            pltpu.SMEM((TGT * SRC + 2,), jnp.int32),
            pltpu.SMEM((TGT * SRC + 2,), jnp.int32),
            pltpu.SMEM((TGT * SRC + 2,), F32),
            pltpu.VMEM((LEAF, LEAF), BF),
            pltpu.VMEM((LEAF, LEAF), BF),
            pltpu.VMEM((LEAF, LEAF), BF),
            pltpu.VMEM((LEAF, LEAF), BF),
            pltpu.VMEM((6, PARTS, F, COLS), F32),
            pltpu.VMEM((XS, F, COLS), F32),
            pltpu.SemaphoreType.DMA((7,)),
        ],
        compiler_params=pltpu.CompilerParams(vmem_limit_bytes=48 << 20),
        name="near",
    )(times, logs, cloud, tgt)


def fold_kernel(
    part, values, interp,
    out,
    first, last, int_v,
    load_sem, first_ss, first_rs, last_ss, last_rs,
):
    g = lax.axis_index("leaf")
    h = lax.axis_index("help")
    x = lax.div(h, 2)
    core = lax.rem(h, 2)

    def x_at(d):
        return lax.rem(x + d, XS)

    def beside(way):
        return x_at(1 if way == 0 else 3)

    def to(way):
        return beside(way) * 2 + core

    barrier = pltpu.get_barrier_semaphore()

    for way in range(2):
        pl.semaphore_signal(barrier, inc=1, device_id=(g, to(way)), device_id_type=MESH)

    load = pltpu.make_async_copy(interp, int_v, load_sem)
    load.start()
    pl.semaphore_wait(barrier, 2)

    def first_copy(way):
        src = part.at[x_at(2) * OWN + way]
        return remote(src, first.at[way], first_ss.at[way], first_rs.at[way], g, to(way))

    def plain_copy(way):
        src = part.at[beside(way) * OWN + 1 - way]
        dst = last.at[way, 1 - way]
        return remote(src, dst, last_ss.at[way, 0], last_rs.at[way, 0], g, to(way))

    def sum_copy(way):
        dst = last.at[way, way]
        return remote(first.at[way], dst, last_ss.at[way, 1], last_rs.at[way, 1], g, to(way))

    for way in range(2):
        first_copy(way).start()
    for way in range(2):
        plain_copy(way).start()
    load.wait()
    spans = [slice(j * LEAF, (j + 1) * LEAF) for j in range(OWN)]
    for j in range(OWN):
        out[:, spans[j]] = part[x * OWN + j] + product3(values[...], int_v[j], mul_t)
    for way in range(2):
        first_copy(way).wait_recv()
        first[way] += part[beside(way) * OWN + way]
        sum_copy(way).start()

    for way in range(2):
        plain_copy(way).wait_recv()
        out[:, spans[1 - way]] += last[way, 1 - way]
    for way in range(2):
        sum_copy(way).wait_recv()
        out[:, spans[way]] += last[way, way]
    for way in range(2):
        first_copy(way).wait_send()
        plain_copy(way).wait_send()
        sum_copy(way).wait_send()


def fold(part, values, interp):
    vmem = pl.BlockSpec(memory_space=pltpu.VMEM)
    anym = pl.BlockSpec(memory_space=pl.ANY)
    dma = pltpu.SemaphoreType.DMA
    return pl.pallas_call(
        fold_kernel,
        out_shape=jax.ShapeDtypeStruct((R, COLS), F32),
        in_specs=[vmem, vmem, anym],
        out_specs=vmem,
        scratch_shapes=[
            pltpu.VMEM((2, R, LEAF), F32),
            pltpu.VMEM((2, OWN, R, LEAF), F32),
            pltpu.VMEM((OWN, LEAF, SK), F32),
            dma,
            dma((2,)), dma((2,)), dma((2, 2)), dma((2, 2)),
        ],
        compiler_params=pltpu.CompilerParams(
            collective_id=1, has_side_effects=True, vmem_limit_bytes=32 << 20
        ),
        name="fold",
    )(part, values, interp)


def shards(
    points, weights, interp, transfer, near_count, near_src, skel_group, skel_node, far_nodes
):
    g = lax.axis_index("leaf")
    x = lax.axis_index("help") // 2
    listed = jnp.where(lax.iota(jnp.int32, NEAR)[None, :] < near_count[0][:, None], near_src, -1)
    cloud, tgt, metas, values = spread(
        points, weights, interp, transfer, skel_group, skel_node, far_nodes.T, listed
    )
    slots = metas.reshape(TGT, 1, NEAR)
    step = lax.iota(jnp.int32, SRC)
    ids = (g - 1 + step // 4) * 16 + x * 4 + step % 4
    ids = jnp.where(ids < 0, -2, ids)
    times = jnp.sum((slots == ids[None, :, None]).astype(jnp.int32), axis=2).reshape(-1)
    logs = jnp.log2(jnp.maximum(times, 1).astype(F32))
    part = near(times, logs, cloud, tgt)
    return fold(part, values, interp)


def solution(mesh):
    placed = (
        P(None, ("leaf", "help")),
        P(None, ("leaf", "help")),
        P(("leaf", "help"), None, None),
        P(),
        P("leaf", "help"),
        P(("leaf", "help"), None),
        P("leaf", None),
        P(),
        P(),
    )
    return jax.shard_map(
        shards, mesh=mesh, in_specs=placed, out_specs=P(None, ("leaf", "help")), check_vma=False
    )
```

```python
import jax
import jax.numpy as jnp
from jax import lax
from jax.experimental import pallas as pl
from jax.experimental.pallas import tpu as pltpu
from jax.sharding import PartitionSpec as P

F = 64
R = 256
LEAF = 512
SK = 256
NEAR = 32
GROUPS = 16
HELP = 8
OWN = 2
COLS = OWN * LEAF
XS = 4
LEVELS = 4
UPPER = 14
STARTS = (0, 16, 24, 28)
NODES = 30
ROWS = R // HELP
PROWS = F // HELP
PARTS = 1 + R // F
ROOT = 0.8493218002880191
PEAK = 5.770780163555854

BF = jnp.bfloat16
F32 = jnp.float32
MESH = pl.DeviceIdType.MESH


def halves(value):
    high = value.astype(BF)
    return high, (value - high.astype(F32)).astype(BF)


def mul(left, right):
    return jnp.dot(left, right, preferred_element_type=F32)


def mul_t(left, right):
    return lax.dot_general(left, right, (((1,), (1,)), ((), ())), preferred_element_type=F32)


def product3(left, right, dot=mul):
    left_hi, left_lo = halves(left)
    right_hi, right_lo = halves(right)
    return dot(left_hi, right_hi) + dot(left_lo, right_hi) + dot(left_hi, right_lo)


def stacked_halves(pts):
    scaled = pts * ROOT
    high = scaled.astype(BF).astype(F32)
    low = (scaled - high).astype(BF).astype(F32)
    return jnp.concatenate([high, low], axis=0)


def target_side(both):
    high, low = both[:F], both[F:]
    whole = high + low
    own = PEAK - 0.5 * jnp.sum(whole * whole, axis=0, keepdims=True)
    high, low = high.astype(BF), low.astype(BF)
    return jnp.concatenate([high, high, low, low], axis=0), own


def source_side(both):
    turned = both.T
    whole = turned[:, :F] + turned[:, F:]
    own = PEAK - 0.5 * jnp.sum(whole * whole, axis=1, keepdims=True)
    turned = turned.astype(BF)
    return jnp.concatenate([turned, turned], axis=1), own


def remote(src, dst, send, recv, group, helper):
    return pltpu.make_async_remote_copy(
        src_ref=src,
        dst_ref=dst,
        send_sem=send,
        recv_sem=recv,
        device_id=(group, helper),
        device_id_type=MESH,
    )


def spread_kernel(
    pts, wts, interp, transfer, skg, skn, far, meta,
    cloud, tgt, metas, v_out,
    pts_v, wts_v, int_v, tr, skg_v, skn_v, far_s,
    ps_send, ps_buf, us_send, us_buf, lp_send, lp_buf, lu_send, p_buf, tier_u, tier_z, v_buf,
    load_sem, y_send, y_recv, f_send, f_recv, s_send, s_recv, own_sem,
    t_send, t_recv, m_send, m_recv,
    ps_ss, ps_rs, us_ss, us_rs, lp_ss, lp_rs, lu_ss, lu_rs, p_ss, p_rs, v_ss, v_rs,
):
    g = lax.axis_index("leaf")
    h = lax.axis_index("help")
    x = lax.div(h, 2)
    core = lax.rem(h, 2)
    sib = h + 1 - 2 * core
    after = lax.rem(g + 1, GROUPS)
    before = lax.rem(g + GROUPS - 1, GROUPS)

    def helper_at(d):
        return lax.rem(h + d, HELP)

    def group_at(d):
        return lax.rem(g + d, GROUPS)

    barrier = pltpu.get_barrier_semaphore()

    @pl.loop(1, HELP)
    def _(d):
        pl.semaphore_signal(barrier, inc=1, device_id=(g, helper_at(d)), device_id_type=MESH)

    @pl.loop(1, GROUPS)
    def _(d):
        pl.semaphore_signal(barrier, inc=1, device_id=(group_at(d), h), device_id_type=MESH)

    pairs = (
        (pts, pts_v), (skg, skg_v), (wts, wts_v), (interp, int_v),
        (skn, skn_v), (transfer, tr), (far, far_s),
    )
    loads = [
        pltpu.make_async_copy(src, dst, load_sem.at[i]) for i, (src, dst) in enumerate(pairs)
    ]
    for copy in loads:
        copy.start()

    def part(i):
        return pts if i == 0 else wts.at[pl.ds(F * (i - 1), F)]

    def y_copy(way, i):
        where = after if way == 0 else before
        return remote(
            part(i), cloud.at[2 * way, core, i], y_send.at[way, i], y_recv.at[way, i], where, h
        )

    def f_copy(way, i):
        spot = cloud.at[2 * way, core, i]
        return remote(spot, spot, f_send.at[way, i], f_recv.at[way, i], g, sib)

    sends = (g < GROUPS - 1, g > 0)

    def y_start(i):
        for way in range(2):
            pl.when(sends[way])(y_copy(way, i).start)

    def f_start(i):
        for way in range(2):

            @pl.when(sends[1 - way])
            def _(way=way):
                y_copy(way, i).wait_recv()
                f_copy(way, i).start()

    def s_copy(i):
        return remote(part(i), cloud.at[1, core, i], s_send.at[i], s_recv.at[i], g, sib)

    def own_copy(i):
        src = pts_v if i == 0 else wts_v.at[pl.ds(F * (i - 1), F)]
        return pltpu.make_async_copy(src, cloud.at[1, core, i], own_sem.at[i])

    def x_at(d):
        return lax.rem(x + d, XS) * 2 + core

    def t_copy(d):
        return remote(pts, tgt.at[x], t_send.at[d], t_recv.at[d], g, x_at(d))

    def m_copy(d):
        return remote(meta, metas.at[x], m_send.at[d], m_recv.at[d], g, x_at(d))

    own_t = pltpu.make_async_copy(pts_v, tgt.at[x], own_sem.at[PARTS])
    own_m = pltpu.make_async_copy(meta, metas.at[x], own_sem.at[PARTS + 1])

    loads[0].wait()
    loads[1].wait()
    picks = skg_v[...] - h * COLS
    onehot = (lax.broadcasted_iota(jnp.int32, (COLS, SK), 0) == picks).astype(BF)
    own_pts = pts_v[...]
    first = own_pts.astype(BF)
    rest = own_pts - first.astype(F32)
    second, third = halves(rest)
    chosen = mul(first, onehot) + mul(second, onehot) + mul(third, onehot)
    ps_send[...] = chosen.reshape(HELP, PROWS, SK)

    loads[2].wait()
    loads[3].wait()
    up = product3(wts_v[...], int_v[...].reshape(COLS, SK))
    us_send[...] = up.reshape(HELP, ROWS, SK)

    pl.semaphore_wait(barrier, HELP + GROUPS - 2)

    def ps_copy(d):
        to = helper_at(d)
        return remote(ps_send.at[to], ps_buf.at[h], ps_ss.at[d], ps_rs.at[d], g, to)

    def us_copy(d):
        to = helper_at(d)
        return remote(us_send.at[to], us_buf.at[h], us_ss.at[d], us_rs.at[d], g, to)

    def lp_copy(d):
        return remote(lp_send, lp_buf.at[g], lp_ss.at[d], lp_rs.at[d], group_at(d), h)

    def lu_copy(d):
        return remote(lu_send, tier_u.at[g], lu_ss.at[d], lu_rs.at[d], group_at(d), h)

    def p_copy(d):
        return remote(lp_buf, p_buf.at[h], p_ss.at[d], p_rs.at[d], g, helper_at(d))

    def v_copy(d):
        return remote(v_buf.at[h], v_buf.at[h], v_ss.at[d], v_rs.at[d], g, helper_at(d))

    @pl.loop(1, HELP)
    def _(d):
        us_copy(d).start()
        ps_copy(d).start()

    y_start(0)
    @pl.loop(1, HELP)
    def _(d):
        us_copy(d).wait_recv()

    us_buf[h] = us_send[h]
    total = us_buf[0]
    for i in range(1, HELP):
        total = total + us_buf[i]
    lu_send[...] = total
    tier_u[g] = total

    @pl.loop(1, GROUPS)
    def _(d):
        lu_copy(d).start()

    @pl.loop(1, HELP)
    def _(d):
        ps_copy(d).wait_recv()

    ps_buf[h] = ps_send[h]
    total = ps_buf[0]
    for i in range(1, HELP):
        total = total + ps_buf[i]
    lp_send[...] = total
    lp_buf[g] = total

    @pl.loop(1, GROUPS)
    def _(d):
        lp_copy(d).start()

    for d in range(1, XS):
        t_copy(d).start()
        m_copy(d).start()
    for i in range(PARTS):
        s_copy(i).start()
        own_copy(i).start()
    own_t.start()
    own_m.start()
    y_start(1)
    y_start(2)

    @pl.loop(1, GROUPS)
    def _(d):
        lp_copy(d).wait_recv()

    @pl.loop(1, HELP)
    def _(d):
        p_copy(d).start()

    y_start(3)
    p_buf[h] = lp_buf[...]

    @pl.loop(1, GROUPS)
    def _(d):
        lu_copy(d).wait_recv()

    y_start(4)

    for copy in loads[4:]:
        copy.wait()

    @pl.loop(0, UPPER, unroll=2)
    def _(r):
        both = jnp.concatenate([tier_u[2 * r], tier_u[2 * r + 1]], axis=1)
        tier_u[GROUPS + r] = product3(both, tr[r])

    f_start(0)

    @pl.loop(1, HELP)
    def _(d):
        p_copy(d).wait_recv()

    @pl.loop(0, GROUPS)
    def _(n):
        tier_z[n] = stacked_halves(p_buf[:, n].reshape(F, SK)).astype(BF)

    rows = lax.broadcasted_iota(jnp.int32, (2 * SK, SK), 0)

    @pl.loop(0, UPPER, unroll=2)
    def _(r):
        both = jnp.concatenate([tier_z[2 * r], tier_z[2 * r + 1]], axis=1)
        pick = (rows == skn_v[pl.ds(r, 1), :]).astype(BF)
        tier_z[GROUPS + r] = mul(both, pick).astype(BF)

    f_start(1)
    sums = []
    for level in range(LEVELS):
        q = STARTS[level] + lax.shift_right_logical(g, level)
        right, target_own = target_side(tier_z[q].astype(F32))
        nodes = [STARTS[level] + far_s[slot, q] for slot in range(4)]
        both = jnp.concatenate([tier_z[node] for node in nodes], axis=1).astype(F32)
        left, source_own = source_side(both)
        block = jnp.exp2(mul(left, right) + source_own + target_own)
        values = jnp.concatenate([tier_u[node] for node in nodes], axis=1)
        sums.append(product3(values, block))
    f_start(2)
    local = sums[LEVELS - 1]
    for level in range(LEVELS - 1, 0, -1):
        r = STARTS[level] - GROUPS + lax.shift_right_logical(g, level)
        side = lax.rem(lax.shift_right_logical(g, level - 1), 2)
        half = tr[r, pl.ds(pl.multiple_of(side * SK, SK), SK), :]
        local = sums[level - 1] + product3(local, half, mul_t)
    v_buf[h] = local

    @pl.loop(1, HELP)
    def _(d):
        v_copy(d).start()

    for i in range(3, PARTS):
        f_start(i)

    @pl.loop(1, HELP)
    def _(d):
        v_copy(d).wait_recv()

    v_out[...] = v_buf[...].reshape(R, SK)

    for i in range(PARTS):
        for way in range(2):
            pl.when(sends[1 - way])(f_copy(way, i).wait)
            pl.when(sends[way])(y_copy(way, i).wait_send)
        s_copy(i).wait()
        own_copy(i).wait()
    for d in range(1, XS):
        t_copy(d).wait()
        m_copy(d).wait()
    own_t.wait()
    own_m.wait()

    @pl.loop(1, HELP)
    def _(d):
        ps_copy(d).wait_send()
        us_copy(d).wait_send()
        p_copy(d).wait_send()
        v_copy(d).wait_send()

    @pl.loop(1, GROUPS)
    def _(d):
        lp_copy(d).wait_send()
        lu_copy(d).wait_send()


def spread(points, weights, interp, transfer, skel_group, skel_node, far_slots, meta):
    vmem = pl.BlockSpec(memory_space=pltpu.VMEM)
    anym = pl.BlockSpec(memory_space=pl.ANY)
    dma = pltpu.SemaphoreType.DMA
    return pl.pallas_call(
        spread_kernel,
        out_shape=(
            jax.ShapeDtypeStruct((3, 2, PARTS, F, COLS), F32),
            jax.ShapeDtypeStruct((XS, F, COLS), F32),
            jax.ShapeDtypeStruct((XS, OWN, NEAR), jnp.int32),
            jax.ShapeDtypeStruct((R, SK), F32),
        ),
        in_specs=[anym] * 8,
        out_specs=(anym, anym, anym, vmem),
        scratch_shapes=[
            pltpu.VMEM((F, COLS), F32),
            pltpu.VMEM((R, COLS), F32),
            pltpu.VMEM((OWN, LEAF, SK), F32),
            pltpu.VMEM((UPPER, 2 * SK, SK), F32),
            pltpu.VMEM((1, SK), jnp.int32),
            pltpu.VMEM((UPPER, SK), jnp.int32),
            pltpu.SMEM((4, NODES), jnp.int32),
            pltpu.VMEM((HELP, PROWS, SK), F32),
            pltpu.VMEM((HELP, PROWS, SK), F32),
            pltpu.VMEM((HELP, ROWS, SK), F32),
            pltpu.VMEM((HELP, ROWS, SK), F32),
            pltpu.VMEM((PROWS, SK), F32),
            pltpu.VMEM((GROUPS, PROWS, SK), F32),
            pltpu.VMEM((ROWS, SK), F32),
            pltpu.VMEM((HELP, GROUPS, PROWS, SK), F32),
            pltpu.VMEM((NODES, ROWS, SK), F32),
            pltpu.VMEM((NODES, 2 * F, SK), BF),
            pltpu.VMEM((HELP, ROWS, SK), F32),
            dma((7,)),
            dma((2, PARTS)), dma((2, PARTS)),
            dma((2, PARTS)), dma((2, PARTS)),
            dma((PARTS,)), dma((PARTS,)),
            dma((PARTS + 2,)),
            dma((XS,)), dma((XS,)),
            dma((XS,)), dma((XS,)),
            dma((HELP,)), dma((HELP,)),
            dma((HELP,)), dma((HELP,)),
            dma((GROUPS,)), dma((GROUPS,)),
            dma((GROUPS,)), dma((GROUPS,)),
            dma((HELP,)), dma((HELP,)),
            dma((HELP,)), dma((HELP,)),
        ],
        compiler_params=pltpu.CompilerParams(
            collective_id=0, has_side_effects=True, vmem_limit_bytes=60 << 20
        ),
        name="spread",
    )(points, weights, interp, transfer, skel_group, skel_node, far_slots, meta)


SRC = 3 * 2 * OWN
TGT = XS * OWN
CUT = 2


def near_kernel(
    times, logs, cloud, tgt, part,
    w_hl, left, source_own, right, target_own,
    list_t, list_s, list_log, hi_a, lo_a, hi_b, lo_b, cloud_v, tgt_v, sems,
):
    def cloud_copy(pair):
        step, core = lax.div(pair, 2), lax.rem(pair, 2)
        return pltpu.make_async_copy(cloud.at[step, core], cloud_v.at[pair], sems.at[pair])

    tgt_copy = pltpu.make_async_copy(tgt, tgt_v, sems.at[6])
    tgt_copy.start()
    for pair in range(6):
        cloud_copy(pair).start()
    tgt_copy.wait()
    @pl.loop(0, XS)
    def _(at):
        for j in range(OWN):
            factor, own = source_side(stacked_halves(tgt_v[at, :, j * LEAF:(j + 1) * LEAF]))
            right[at * OWN + j] = factor
            target_own[at * OWN + j] = jnp.broadcast_to(own, (LEAF, 128))
            part[at * OWN + j] = jnp.zeros((R, LEAF), F32)

    @pl.loop(0, 6)
    def _(pair):
        cloud_copy(pair).wait()
        for j in range(OWN):
            span = slice(j * LEAF, (j + 1) * LEAF)
            s = pair * OWN + j
            for i in range(R // F):
                high, low = halves(cloud_v[pair, 1 + i, :, span])
                w_hl[s, i * F:(i + 1) * F, :] = high
                w_hl[s, R + i * F:R + (i + 1) * F, :] = low
            factor, own = target_side(stacked_halves(cloud_v[pair, 0, :, span]))
            left[s] = factor
            source_own[s] = jnp.broadcast_to(own, (8, LEAF))

    def note(k, n):
        list_t[n] = lax.div(k, SRC)
        list_s[n] = lax.rem(k, SRC)
        list_log[n] = logs[k]
        return n + (times[k] > 0).astype(jnp.int32)

    count = lax.fori_loop(0, TGT * SRC, note, jnp.int32(0))
    for extra in range(2):
        list_t[count + extra] = 0
        list_s[count + extra] = 0
        list_log[count + extra] = jnp.float32(-1e30)

    def produce(i, hi, lo):
        t, s = list_t[i], list_s[i]
        shift = source_own[s, 0:1, :] + list_log[i]
        for c in range(CUT):
            n = LEAF // CUT
            span = slice(c * n, (c + 1) * n)
            cross = mul(right[t, span], left[s])
            own = target_own[t, span]
            block = jnp.exp2(cross + jnp.concatenate([own] * 4, axis=1) + shift)
            high, low = halves(block)
            hi[span] = high
            lo[span] = low

    def consume(i, hi, lo):
        t, s = list_t[i], list_s[i]
        for c in range(CUT):
            n = LEAF // CUT
            span = slice(c * n, (c + 1) * n)
            two = mul_t(w_hl[s], hi[span])
            part[t, :, span] += two[:R] + two[R:] + mul_t(w_hl[s, :R], lo[span])

    produce(0, hi_a, lo_a)

    @pl.loop(0, lax.div(count + 1, 2))
    def _(k):
        produce(2 * k + 1, hi_b, lo_b)
        consume(2 * k, hi_a, lo_a)
        produce(jnp.minimum(2 * k + 2, count), hi_a, lo_a)
        consume(2 * k + 1, hi_b, lo_b)


def near(times, logs, cloud, tgt):
    vmem = pl.BlockSpec(memory_space=pltpu.VMEM)
    anym = pl.BlockSpec(memory_space=pl.ANY)
    smem = pl.BlockSpec(memory_space=pltpu.SMEM)
    return pl.pallas_call(
        near_kernel,
        out_shape=jax.ShapeDtypeStruct((TGT, R, LEAF), F32),
        in_specs=[smem, smem, anym, anym],
        out_specs=vmem,
        scratch_shapes=[
            pltpu.VMEM((SRC, 2 * R, LEAF), BF),
            pltpu.VMEM((SRC, 4 * F, LEAF), BF),
            pltpu.VMEM((SRC, 8, LEAF), F32),
            pltpu.VMEM((TGT, LEAF, 4 * F), BF),
            pltpu.VMEM((TGT, LEAF, 128), F32),
            pltpu.SMEM((TGT * SRC + 2,), jnp.int32),
            pltpu.SMEM((TGT * SRC + 2,), jnp.int32),
            pltpu.SMEM((TGT * SRC + 2,), F32),
            pltpu.VMEM((LEAF, LEAF), BF),
            pltpu.VMEM((LEAF, LEAF), BF),
            pltpu.VMEM((LEAF, LEAF), BF),
            pltpu.VMEM((LEAF, LEAF), BF),
            pltpu.VMEM((6, PARTS, F, COLS), F32),
            pltpu.VMEM((XS, F, COLS), F32),
            pltpu.SemaphoreType.DMA((7,)),
        ],
        compiler_params=pltpu.CompilerParams(vmem_limit_bytes=48 << 20),
        name="near",
    )(times, logs, cloud, tgt)


def fold_kernel(
    logs, part, values, interp, cloud, pts,
    out,
    first, last, int_v, cloud_v, pts_v,
    w_hl, left, source_own, right, target_own, hi, lo,
    load_sem, first_ss, first_rs, last_ss, last_rs,
):
    g = lax.axis_index("leaf")
    h = lax.axis_index("help")
    x = lax.div(h, 2)
    core = lax.rem(h, 2)

    def x_at(d):
        return lax.rem(x + d, XS)

    def beside(way):
        return x_at(1 if way == 0 else 3)

    def to(way):
        return beside(way) * 2 + core

    barrier = pltpu.get_barrier_semaphore()

    for way in range(2):
        pl.semaphore_signal(barrier, inc=1, device_id=(g, to(way)), device_id_type=MESH)

    def cloud_copy(pair):
        step, at = lax.div(pair, 2), lax.rem(pair, 2)
        return pltpu.make_async_copy(cloud.at[step, at], cloud_v.at[pair], load_sem.at[pair])

    pts_load = pltpu.make_async_copy(pts, pts_v, load_sem.at[6])
    int_load = pltpu.make_async_copy(interp, int_v, load_sem.at[7])
    pts_load.start()
    for pair in range(6):
        cloud_copy(pair).start()
    int_load.start()
    pl.semaphore_wait(barrier, 2)

    def first_copy(way):
        src = part.at[x_at(2) * OWN + way]
        return remote(src, first.at[way], first_ss.at[way], first_rs.at[way], g, to(way))

    def plain_copy(way):
        src = part.at[beside(way) * OWN + 1 - way]
        dst = last.at[way, 1 - way]
        return remote(src, dst, last_ss.at[way, 0], last_rs.at[way, 0], g, to(way))

    def sum_copy(way):
        dst = last.at[way, way]
        return remote(first.at[way], dst, last_ss.at[way, 1], last_rs.at[way, 1], g, to(way))

    for way in range(2):
        first_copy(way).start()
    for way in range(2):
        plain_copy(way).start()

    spans = [slice(j * LEAF, (j + 1) * LEAF) for j in range(OWN)]
    pts_load.wait()
    for t in range(OWN):
        factor, own = source_side(stacked_halves(pts_v[:, spans[t]]))
        right[t] = factor
        target_own[t] = jnp.broadcast_to(own, (LEAF, 128))
    int_load.wait()
    for j in range(OWN):
        out[:, spans[j]] = product3(values[...], int_v[j], mul_t)

    def tiles(pair):
        cloud_copy(pair).wait()
        step = lax.div(pair, 2)
        missing = ((step == 0) & (g == 0)) | ((step == 2) & (g == GROUPS - 1))
        for j in range(OWN):
            for i in range(R // F):
                value = jnp.where(missing, 0.0, cloud_v[pair, 1 + i, :, spans[j]])
                high, low = halves(value)
                w_hl[j, i * F:(i + 1) * F, :] = high
                w_hl[j, R + i * F:R + (i + 1) * F, :] = low
            value = jnp.where(missing, 0.0, cloud_v[pair, 0, :, spans[j]])
            factor, own = target_side(stacked_halves(value))
            left[j] = factor
            source_own[j] = jnp.broadcast_to(own, (8, LEAF))
        for j in range(OWN):
            for t in range(OWN):
                shift = source_own[j, 0:1, :] + logs[t * SRC + pair * OWN + j]
                for c in range(CUT):
                    n = LEAF // CUT
                    span = slice(c * n, (c + 1) * n)
                    cross = mul(right[t, span], left[j])
                    own = target_own[t, span]
                    block = jnp.exp2(cross + jnp.concatenate([own] * 4, axis=1) + shift)
                    high, low = halves(block)
                    hi[j, t, span] = high
                    lo[j, t, span] = low
        for j in range(OWN):
            for t in range(OWN):
                for c in range(CUT):
                    n = LEAF // CUT
                    span = slice(c * n, (c + 1) * n)
                    where = slice(t * LEAF + c * n, t * LEAF + (c + 1) * n)
                    two = mul_t(w_hl[j], hi[j, t, span])
                    out[:, where] += two[:R] + two[R:] + mul_t(w_hl[j, :R], lo[j, t, span])

    pl.loop(0, 3)(tiles)
    for way in range(2):
        first_copy(way).wait_recv()
        first[way] += part[beside(way) * OWN + way]
        sum_copy(way).start()
    pl.loop(3, 6)(tiles)

    for way in range(2):
        plain_copy(way).wait_recv()
        out[:, spans[1 - way]] += last[way, 1 - way]
    for way in range(2):
        sum_copy(way).wait_recv()
        out[:, spans[way]] += last[way, way]
    for way in range(2):
        first_copy(way).wait_send()
        plain_copy(way).wait_send()
        sum_copy(way).wait_send()


def fold(logs, part, values, interp, cloud, points):
    vmem = pl.BlockSpec(memory_space=pltpu.VMEM)
    smem = pl.BlockSpec(memory_space=pltpu.SMEM)
    anym = pl.BlockSpec(memory_space=pl.ANY)
    dma = pltpu.SemaphoreType.DMA
    return pl.pallas_call(
        fold_kernel,
        out_shape=jax.ShapeDtypeStruct((R, COLS), F32),
        in_specs=[smem, vmem, vmem, anym, anym, anym],
        out_specs=vmem,
        scratch_shapes=[
            pltpu.VMEM((2, R, LEAF), F32),
            pltpu.VMEM((2, OWN, R, LEAF), F32),
            pltpu.VMEM((OWN, LEAF, SK), F32),
            pltpu.VMEM((6, PARTS, F, COLS), F32),
            pltpu.VMEM((F, COLS), F32),
            pltpu.VMEM((OWN, 2 * R, LEAF), BF),
            pltpu.VMEM((OWN, 4 * F, LEAF), BF),
            pltpu.VMEM((OWN, 8, LEAF), F32),
            pltpu.VMEM((OWN, LEAF, 4 * F), BF),
            pltpu.VMEM((OWN, LEAF, 128), F32),
            pltpu.VMEM((OWN, OWN, LEAF, LEAF), BF),
            pltpu.VMEM((OWN, OWN, LEAF, LEAF), BF),
            dma((8,)),
            dma((2,)), dma((2,)), dma((2, 2)), dma((2, 2)),
        ],
        compiler_params=pltpu.CompilerParams(
            collective_id=1, has_side_effects=True, vmem_limit_bytes=44 << 20
        ),
        name="fold",
    )(logs, part, values, interp, cloud, points)


def shards(
    points, weights, interp, transfer, near_count, near_src, skel_group, skel_node, far_nodes
):
    g = lax.axis_index("leaf")
    x = lax.axis_index("help") // 2
    listed = jnp.where(lax.iota(jnp.int32, NEAR)[None, :] < near_count[0][:, None], near_src, -1)
    cloud, tgt, metas, values = spread(
        points, weights, interp, transfer, skel_group, skel_node, far_nodes.T, listed
    )
    slots = metas.reshape(TGT, 1, NEAR)
    step = lax.iota(jnp.int32, SRC)
    ids = (g - 1 + step // 4) * 16 + x * 4 + step % 4
    ids = jnp.where(ids < 0, -2, ids)
    times = jnp.sum((slots == ids[None, :, None]).astype(jnp.int32), axis=2)
    logs = jnp.log2(jnp.maximum(times, 1).astype(F32))
    own_logs = jnp.where(times > 0, logs, -1e30)
    own_logs = lax.dynamic_slice_in_dim(own_logs, x * OWN, OWN, 0).reshape(-1)
    away = lax.iota(jnp.int32, TGT)[:, None] // OWN != x
    part = near(jnp.where(away, times, 0).reshape(-1), logs.reshape(-1), cloud, tgt)
    return fold(own_logs, part, values, interp, cloud, points)


def solution(mesh):
    placed = (
        P(None, ("leaf", "help")),
        P(None, ("leaf", "help")),
        P(("leaf", "help"), None, None),
        P(),
        P("leaf", "help"),
        P(("leaf", "help"), None),
        P("leaf", None),
        P(),
        P(),
    )
    return jax.shard_map(
        shards, mesh=mesh, in_specs=placed, out_specs=P(None, ("leaf", "help")), check_vma=False
    )
```

```python
import jax
import jax.numpy as jnp
from jax import lax
from jax.experimental import pallas as pl
from jax.experimental.pallas import tpu as pltpu
from jax.sharding import PartitionSpec as P

F = 64
R = 256
LEAF = 512
SK = 256
NEAR = 32
GROUPS = 16
HELP = 8
OWN = 2
COLS = OWN * LEAF
XS = 4
LEVELS = 4
UPPER = 14
STARTS = (0, 16, 24, 28)
NODES = 30
ROWS = R // HELP
PROWS = F // HELP
PARTS = 1 + R // F
ROOT = 0.8493218002880191
PEAK = 5.770780163555854

BF = jnp.bfloat16
F32 = jnp.float32
MESH = pl.DeviceIdType.MESH


def halves(value):
    high = value.astype(BF)
    return high, (value - high.astype(F32)).astype(BF)


def mul(left, right):
    return jnp.dot(left, right, preferred_element_type=F32)


def mul_t(left, right):
    return lax.dot_general(left, right, (((1,), (1,)), ((), ())), preferred_element_type=F32)


def product3(left, right, dot=mul):
    left_hi, left_lo = halves(left)
    right_hi, right_lo = halves(right)
    return dot(left_hi, right_hi) + dot(left_lo, right_hi) + dot(left_hi, right_lo)


def stacked_halves(pts):
    scaled = pts * ROOT
    high = scaled.astype(BF).astype(F32)
    low = (scaled - high).astype(BF).astype(F32)
    return jnp.concatenate([high, low], axis=0)


def target_side(both):
    high, low = both[:F], both[F:]
    whole = high + low
    own = PEAK - 0.5 * jnp.sum(whole * whole, axis=0, keepdims=True)
    high, low = high.astype(BF), low.astype(BF)
    return jnp.concatenate([high, high, low, low], axis=0), own


def source_side(both):
    turned = both.T
    whole = turned[:, :F] + turned[:, F:]
    own = PEAK - 0.5 * jnp.sum(whole * whole, axis=1, keepdims=True)
    turned = turned.astype(BF)
    return jnp.concatenate([turned, turned], axis=1), own


def remote(src, dst, send, recv, group, helper):
    return pltpu.make_async_remote_copy(
        src_ref=src,
        dst_ref=dst,
        send_sem=send,
        recv_sem=recv,
        device_id=(group, helper),
        device_id_type=MESH,
    )


def spread_kernel(
    pts, wts, interp, transfer, skg, skn, far, meta,
    cloud, tgt, metas, v_out,
    pts_v, wts_v, int_v, tr, skg_v, skn_v, far_s,
    ps_send, ps_buf, us_send, us_buf, lp_send, lp_buf, lu_send, p_buf, tier_u, tier_z, picked, v_buf,
    load_sem, y_send, y_recv, f_send, f_recv, s_send, s_recv, own_sem,
    t_send, t_recv, m_send, m_recv,
    ps_ss, ps_rs, us_ss, us_rs, lp_ss, lp_rs, lu_ss, lu_rs, p_ss, p_rs, v_ss, v_rs,
):
    g = lax.axis_index("leaf")
    h = lax.axis_index("help")
    x = lax.div(h, 2)
    core = lax.rem(h, 2)
    sib = h + 1 - 2 * core
    after = lax.rem(g + 1, GROUPS)
    before = lax.rem(g + GROUPS - 1, GROUPS)

    def helper_at(d):
        return lax.rem(h + d, HELP)

    def group_at(d):
        return lax.rem(g + d, GROUPS)

    barrier = pltpu.get_barrier_semaphore()

    @pl.loop(1, HELP)
    def _(d):
        pl.semaphore_signal(barrier, inc=1, device_id=(g, helper_at(d)), device_id_type=MESH)

    @pl.loop(1, GROUPS)
    def _(d):
        pl.semaphore_signal(barrier, inc=1, device_id=(group_at(d), h), device_id_type=MESH)

    pairs = (
        (pts, pts_v), (skg, skg_v), (wts, wts_v), (interp, int_v),
        (skn, skn_v), (transfer, tr), (far, far_s),
    )
    loads = [
        pltpu.make_async_copy(src, dst, load_sem.at[i]) for i, (src, dst) in enumerate(pairs)
    ]
    for copy in loads:
        copy.start()

    def part(i):
        return pts if i == 0 else wts.at[pl.ds(F * (i - 1), F)]

    def y_copy(way, i):
        where = after if way == 0 else before
        return remote(
            part(i), cloud.at[2 * way, core, i], y_send.at[way, i], y_recv.at[way, i], where, h
        )

    def f_copy(way, i):
        spot = cloud.at[2 * way, core, i]
        return remote(spot, spot, f_send.at[way, i], f_recv.at[way, i], g, sib)

    sends = (g < GROUPS - 1, g > 0)

    def y_start(i):
        for way in range(2):
            pl.when(sends[way])(y_copy(way, i).start)

    def f_start(i):
        for way in range(2):

            @pl.when(sends[1 - way])
            def _(way=way):
                y_copy(way, i).wait_recv()
                f_copy(way, i).start()

    def s_copy(i):
        return remote(part(i), cloud.at[1, core, i], s_send.at[i], s_recv.at[i], g, sib)

    def own_copy(i):
        src = pts_v if i == 0 else wts_v.at[pl.ds(F * (i - 1), F)]
        return pltpu.make_async_copy(src, cloud.at[1, core, i], own_sem.at[i])

    def x_at(d):
        return lax.rem(x + d, XS) * 2 + core

    def t_copy(d):
        return remote(pts, tgt.at[x], t_send.at[d], t_recv.at[d], g, x_at(d))

    def m_copy(d):
        return remote(meta, metas.at[x], m_send.at[d], m_recv.at[d], g, x_at(d))

    own_t = pltpu.make_async_copy(pts_v, tgt.at[x], own_sem.at[PARTS])
    own_m = pltpu.make_async_copy(meta, metas.at[x], own_sem.at[PARTS + 1])

    loads[0].wait()
    loads[1].wait()
    picks = skg_v[...] - h * COLS
    onehot = (lax.broadcasted_iota(jnp.int32, (COLS, SK), 0) == picks).astype(BF)
    own_pts = pts_v[...]
    first = own_pts.astype(BF)
    rest = own_pts - first.astype(F32)
    second, third = halves(rest)
    chosen = mul(first, onehot) + mul(second, onehot) + mul(third, onehot)
    ps_send[...] = chosen.reshape(HELP, PROWS, SK)

    loads[2].wait()
    loads[3].wait()
    up = product3(wts_v[...], int_v[...].reshape(COLS, SK))
    us_send[...] = up.reshape(HELP, ROWS, SK)

    pl.semaphore_wait(barrier, HELP + GROUPS - 2)

    def ps_copy(d):
        to = helper_at(d)
        return remote(ps_send.at[to], ps_buf.at[h], ps_ss.at[d], ps_rs.at[d], g, to)

    def us_copy(d):
        to = helper_at(d)
        return remote(us_send.at[to], us_buf.at[h], us_ss.at[d], us_rs.at[d], g, to)

    def lp_copy(d):
        return remote(lp_send, lp_buf.at[g], lp_ss.at[d], lp_rs.at[d], group_at(d), h)

    def lu_copy(d):
        return remote(lu_send, tier_u.at[g], lu_ss.at[d], lu_rs.at[d], group_at(d), h)

    def p_copy(d):
        return remote(lp_buf, p_buf.at[h], p_ss.at[d], p_rs.at[d], g, helper_at(d))

    def v_copy(d):
        return remote(v_buf.at[h], v_buf.at[h], v_ss.at[d], v_rs.at[d], g, helper_at(d))

    @pl.loop(1, HELP)
    def _(d):
        ps_copy(d).start()
        us_copy(d).start()

    y_start(0)
    @pl.loop(1, HELP)
    def _(d):
        ps_copy(d).wait_recv()

    ps_buf[h] = ps_send[h]
    total = ps_buf[0]
    for i in range(1, HELP):
        total = total + ps_buf[i]
    lp_send[...] = total
    lp_buf[g] = total

    @pl.loop(1, GROUPS)
    def _(d):
        lp_copy(d).start()

    @pl.loop(1, HELP)
    def _(d):
        us_copy(d).wait_recv()

    us_buf[h] = us_send[h]
    total = us_buf[0]
    for i in range(1, HELP):
        total = total + us_buf[i]
    lu_send[...] = total
    tier_u[g] = total

    @pl.loop(1, GROUPS)
    def _(d):
        lu_copy(d).start()

    for d in range(1, XS):
        t_copy(d).start()
        m_copy(d).start()
    for i in range(PARTS):
        s_copy(i).start()
        own_copy(i).start()
    own_t.start()
    own_m.start()
    y_start(1)
    y_start(2)

    @pl.loop(1, GROUPS)
    def _(d):
        lp_copy(d).wait_recv()

    @pl.loop(1, HELP)
    def _(d):
        p_copy(d).start()

    y_start(3)
    p_buf[h] = lp_buf[...]

    @pl.loop(1, GROUPS)
    def _(d):
        lu_copy(d).wait_recv()

    y_start(4)

    for copy in loads[4:]:
        copy.wait()

    @pl.loop(0, UPPER, unroll=2)
    def _(r):
        both = jnp.concatenate([tier_u[2 * r], tier_u[2 * r + 1]], axis=1)
        tier_u[GROUPS + r] = product3(both, tr[r])

    rows = lax.broadcasted_iota(jnp.int32, (2 * SK, SK), 0)

    @pl.loop(0, UPPER)
    def _(r):
        picked[r] = (rows == skn_v[pl.ds(r, 1), :]).astype(BF)

    f_start(0)

    @pl.loop(1, HELP)
    def _(d):
        p_copy(d).wait_recv()

    @pl.loop(0, GROUPS)
    def _(n):
        tier_z[n] = stacked_halves(p_buf[:, n].reshape(F, SK)).astype(BF)

    @pl.loop(0, UPPER, unroll=2)
    def _(r):
        both = jnp.concatenate([tier_z[2 * r], tier_z[2 * r + 1]], axis=1)
        tier_z[GROUPS + r] = mul(both, picked[r]).astype(BF)

    f_start(1)
    sums = []
    for level in range(LEVELS):
        q = STARTS[level] + lax.shift_right_logical(g, level)
        right, target_own = target_side(tier_z[q].astype(F32))
        nodes = [STARTS[level] + far_s[slot, q] for slot in range(4)]
        both = jnp.concatenate([tier_z[node] for node in nodes], axis=1).astype(F32)
        left, source_own = source_side(both)
        block = jnp.exp2(mul(left, right) + source_own + target_own)
        values = jnp.concatenate([tier_u[node] for node in nodes], axis=1)
        sums.append(product3(values, block))
    f_start(2)
    local = sums[LEVELS - 1]
    for level in range(LEVELS - 1, 0, -1):
        r = STARTS[level] - GROUPS + lax.shift_right_logical(g, level)
        side = lax.rem(lax.shift_right_logical(g, level - 1), 2)
        half = tr[r, pl.ds(pl.multiple_of(side * SK, SK), SK), :]
        local = sums[level - 1] + product3(local, half, mul_t)
    v_buf[h] = local

    @pl.loop(1, HELP)
    def _(d):
        v_copy(d).start()

    for i in range(3, PARTS):
        f_start(i)

    @pl.loop(1, HELP)
    def _(d):
        v_copy(d).wait_recv()

    v_out[...] = v_buf[...].reshape(R, SK)

    for i in range(PARTS):
        for way in range(2):
            pl.when(sends[1 - way])(f_copy(way, i).wait)
            pl.when(sends[way])(y_copy(way, i).wait_send)
        s_copy(i).wait()
        own_copy(i).wait()
    for d in range(1, XS):
        t_copy(d).wait()
        m_copy(d).wait()
    own_t.wait()
    own_m.wait()

    @pl.loop(1, HELP)
    def _(d):
        ps_copy(d).wait_send()
        us_copy(d).wait_send()
        p_copy(d).wait_send()
        v_copy(d).wait_send()

    @pl.loop(1, GROUPS)
    def _(d):
        lp_copy(d).wait_send()
        lu_copy(d).wait_send()


def spread(points, weights, interp, transfer, skel_group, skel_node, far_slots, meta):
    vmem = pl.BlockSpec(memory_space=pltpu.VMEM)
    anym = pl.BlockSpec(memory_space=pl.ANY)
    dma = pltpu.SemaphoreType.DMA
    return pl.pallas_call(
        spread_kernel,
        out_shape=(
            jax.ShapeDtypeStruct((3, 2, PARTS, F, COLS), F32),
            jax.ShapeDtypeStruct((XS, F, COLS), F32),
            jax.ShapeDtypeStruct((XS, OWN, NEAR), jnp.int32),
            jax.ShapeDtypeStruct((R, SK), F32),
        ),
        in_specs=[anym] * 8,
        out_specs=(anym, anym, anym, vmem),
        scratch_shapes=[
            pltpu.VMEM((F, COLS), F32),
            pltpu.VMEM((R, COLS), F32),
            pltpu.VMEM((OWN, LEAF, SK), F32),
            pltpu.VMEM((UPPER, 2 * SK, SK), F32),
            pltpu.VMEM((1, SK), jnp.int32),
            pltpu.VMEM((UPPER, SK), jnp.int32),
            pltpu.SMEM((4, NODES), jnp.int32),
            pltpu.VMEM((HELP, PROWS, SK), F32),
            pltpu.VMEM((HELP, PROWS, SK), F32),
            pltpu.VMEM((HELP, ROWS, SK), F32),
            pltpu.VMEM((HELP, ROWS, SK), F32),
            pltpu.VMEM((PROWS, SK), F32),
            pltpu.VMEM((GROUPS, PROWS, SK), F32),
            pltpu.VMEM((ROWS, SK), F32),
            pltpu.VMEM((HELP, GROUPS, PROWS, SK), F32),
            pltpu.VMEM((NODES, ROWS, SK), F32),
            pltpu.VMEM((NODES, 2 * F, SK), BF),
            pltpu.VMEM((UPPER, 2 * SK, SK), BF),
            pltpu.VMEM((HELP, ROWS, SK), F32),
            dma((7,)),
            dma((2, PARTS)), dma((2, PARTS)),
            dma((2, PARTS)), dma((2, PARTS)),
            dma((PARTS,)), dma((PARTS,)),
            dma((PARTS + 2,)),
            dma((XS,)), dma((XS,)),
            dma((XS,)), dma((XS,)),
            dma((HELP,)), dma((HELP,)),
            dma((HELP,)), dma((HELP,)),
            dma((GROUPS,)), dma((GROUPS,)),
            dma((GROUPS,)), dma((GROUPS,)),
            dma((HELP,)), dma((HELP,)),
            dma((HELP,)), dma((HELP,)),
        ],
        compiler_params=pltpu.CompilerParams(
            collective_id=0, has_side_effects=True, vmem_limit_bytes=60 << 20
        ),
        name="spread",
    )(points, weights, interp, transfer, skel_group, skel_node, far_slots, meta)


SRC = 3 * 2 * OWN
TGT = XS * OWN
CUT = 2


def near_kernel(
    times, logs, cloud, tgt, part,
    w_hl, left, source_own, right, target_own,
    list_t, list_s, list_log, hi_a, lo_a, hi_b, lo_b, cloud_v, tgt_v, sems,
):
    def cloud_copy(pair):
        step, core = lax.div(pair, 2), lax.rem(pair, 2)
        return pltpu.make_async_copy(cloud.at[step, core], cloud_v.at[pair], sems.at[pair])

    tgt_copy = pltpu.make_async_copy(tgt, tgt_v, sems.at[6])
    tgt_copy.start()
    for pair in range(6):
        cloud_copy(pair).start()
    tgt_copy.wait()
    x = lax.div(lax.axis_index("help"), 2)

    @pl.loop(1, XS)
    def _(d):
        at = lax.rem(x + d, XS)
        for j in range(OWN):
            factor, own = source_side(stacked_halves(tgt_v[at, :, j * LEAF:(j + 1) * LEAF]))
            right[at * OWN + j] = factor
            target_own[at * OWN + j] = jnp.broadcast_to(own, (LEAF, 128))
            part[at * OWN + j] = jnp.zeros((R, LEAF), F32)

    @pl.loop(0, 6)
    def _(pair):
        cloud_copy(pair).wait()
        for j in range(OWN):
            span = slice(j * LEAF, (j + 1) * LEAF)
            s = pair * OWN + j
            for i in range(R // F):
                high, low = halves(cloud_v[pair, 1 + i, :, span])
                w_hl[s, i * F:(i + 1) * F, :] = high
                w_hl[s, R + i * F:R + (i + 1) * F, :] = low
            factor, own = target_side(stacked_halves(cloud_v[pair, 0, :, span]))
            left[s] = factor
            source_own[s] = jnp.broadcast_to(own, (8, LEAF))

    def note(k, n):
        list_t[n] = lax.div(k, SRC)
        list_s[n] = lax.rem(k, SRC)
        list_log[n] = logs[k]
        return n + (times[k] > 0).astype(jnp.int32)

    count = lax.fori_loop(0, TGT * SRC, note, jnp.int32(0))
    for extra in range(2):
        list_t[count + extra] = lax.rem(x + 1, XS) * OWN
        list_s[count + extra] = 2 * OWN
        list_log[count + extra] = jnp.float32(-1e30)

    def produce(i, hi, lo):
        t, s = list_t[i], list_s[i]
        shift = source_own[s, 0:1, :] + list_log[i]
        for c in range(CUT):
            n = LEAF // CUT
            span = slice(c * n, (c + 1) * n)
            cross = mul(right[t, span], left[s])
            own = target_own[t, span]
            block = jnp.exp2(cross + jnp.concatenate([own] * 4, axis=1) + shift)
            high, low = halves(block)
            hi[span] = high
            lo[span] = low

    def consume(i, hi, lo):
        t, s = list_t[i], list_s[i]
        for c in range(CUT):
            n = LEAF // CUT
            span = slice(c * n, (c + 1) * n)
            two = mul_t(w_hl[s], hi[span])
            part[t, :, span] += two[:R] + two[R:] + mul_t(w_hl[s, :R], lo[span])

    produce(0, hi_a, lo_a)

    @pl.loop(0, lax.div(count + 1, 2))
    def _(k):
        produce(2 * k + 1, hi_b, lo_b)
        consume(2 * k, hi_a, lo_a)
        produce(jnp.minimum(2 * k + 2, count), hi_a, lo_a)
        consume(2 * k + 1, hi_b, lo_b)


def near(times, logs, cloud, tgt):
    vmem = pl.BlockSpec(memory_space=pltpu.VMEM)
    anym = pl.BlockSpec(memory_space=pl.ANY)
    smem = pl.BlockSpec(memory_space=pltpu.SMEM)
    return pl.pallas_call(
        near_kernel,
        out_shape=jax.ShapeDtypeStruct((TGT, R, LEAF), F32),
        in_specs=[smem, smem, anym, anym],
        out_specs=vmem,
        scratch_shapes=[
            pltpu.VMEM((SRC, 2 * R, LEAF), BF),
            pltpu.VMEM((SRC, 4 * F, LEAF), BF),
            pltpu.VMEM((SRC, 8, LEAF), F32),
            pltpu.VMEM((TGT, LEAF, 4 * F), BF),
            pltpu.VMEM((TGT, LEAF, 128), F32),
            pltpu.SMEM((TGT * SRC + 2,), jnp.int32),
            pltpu.SMEM((TGT * SRC + 2,), jnp.int32),
            pltpu.SMEM((TGT * SRC + 2,), F32),
            pltpu.VMEM((LEAF, LEAF), BF),
            pltpu.VMEM((LEAF, LEAF), BF),
            pltpu.VMEM((LEAF, LEAF), BF),
            pltpu.VMEM((LEAF, LEAF), BF),
            pltpu.VMEM((6, PARTS, F, COLS), F32),
            pltpu.VMEM((XS, F, COLS), F32),
            pltpu.SemaphoreType.DMA((7,)),
        ],
        compiler_params=pltpu.CompilerParams(vmem_limit_bytes=48 << 20),
        name="near",
    )(times, logs, cloud, tgt)


def fold_kernel(
    logs, part, values, interp, cloud, pts,
    out,
    first, last, int_v, cloud_v, pts_v,
    w_hl, left, source_own, right, target_own, hi, lo,
    load_sem, first_ss, first_rs, last_ss, last_rs,
):
    g = lax.axis_index("leaf")
    h = lax.axis_index("help")
    x = lax.div(h, 2)
    core = lax.rem(h, 2)

    def x_at(d):
        return lax.rem(x + d, XS)

    def beside(way):
        return x_at(1 if way == 0 else 3)

    def to(way):
        return beside(way) * 2 + core

    barrier = pltpu.get_barrier_semaphore()

    for way in range(2):
        pl.semaphore_signal(barrier, inc=1, device_id=(g, to(way)), device_id_type=MESH)

    def cloud_copy(pair):
        step, at = lax.div(pair, 2), lax.rem(pair, 2)
        return pltpu.make_async_copy(cloud.at[step, at], cloud_v.at[pair], load_sem.at[pair])

    pts_load = pltpu.make_async_copy(pts, pts_v, load_sem.at[6])
    int_load = pltpu.make_async_copy(interp, int_v, load_sem.at[7])
    pts_load.start()
    for pair in range(6):
        cloud_copy(pair).start()
    int_load.start()
    pl.semaphore_wait(barrier, 2)

    def first_copy(way):
        src = part.at[x_at(2) * OWN + way]
        return remote(src, first.at[way], first_ss.at[way], first_rs.at[way], g, to(way))

    def plain_copy(way):
        src = part.at[beside(way) * OWN + 1 - way]
        dst = last.at[way, 1 - way]
        return remote(src, dst, last_ss.at[way, 0], last_rs.at[way, 0], g, to(way))

    def sum_copy(way):
        dst = last.at[way, way]
        return remote(first.at[way], dst, last_ss.at[way, 1], last_rs.at[way, 1], g, to(way))

    for way in range(2):
        first_copy(way).start()
    for way in range(2):
        plain_copy(way).start()

    spans = [slice(j * LEAF, (j + 1) * LEAF) for j in range(OWN)]
    pts_load.wait()
    for t in range(OWN):
        factor, own = source_side(stacked_halves(pts_v[:, spans[t]]))
        right[t] = factor
        target_own[t] = jnp.broadcast_to(own, (LEAF, 128))
    int_load.wait()
    for j in range(OWN):
        out[:, spans[j]] = product3(values[...], int_v[j], mul_t)

    def tiles(pair):
        cloud_copy(pair).wait()
        step = lax.div(pair, 2)
        missing = ((step == 0) & (g == 0)) | ((step == 2) & (g == GROUPS - 1))
        for j in range(OWN):
            for i in range(R // F):
                value = jnp.where(missing, 0.0, cloud_v[pair, 1 + i, :, spans[j]])
                high, low = halves(value)
                w_hl[j, i * F:(i + 1) * F, :] = high
                w_hl[j, R + i * F:R + (i + 1) * F, :] = low
            value = jnp.where(missing, 0.0, cloud_v[pair, 0, :, spans[j]])
            factor, own = target_side(stacked_halves(value))
            left[j] = factor
            source_own[j] = jnp.broadcast_to(own, (8, LEAF))
        for j in range(OWN):
            for t in range(OWN):
                shift = source_own[j, 0:1, :] + logs[t * SRC + pair * OWN + j]
                for c in range(CUT):
                    n = LEAF // CUT
                    span = slice(c * n, (c + 1) * n)
                    cross = mul(right[t, span], left[j])
                    own = target_own[t, span]
                    block = jnp.exp2(cross + jnp.concatenate([own] * 4, axis=1) + shift)
                    high, low = halves(block)
                    hi[j, t, span] = high
                    lo[j, t, span] = low
        for j in range(OWN):
            for t in range(OWN):
                for c in range(CUT):
                    n = LEAF // CUT
                    span = slice(c * n, (c + 1) * n)
                    where = slice(t * LEAF + c * n, t * LEAF + (c + 1) * n)
                    two = mul_t(w_hl[j], hi[j, t, span])
                    out[:, where] += two[:R] + two[R:] + mul_t(w_hl[j, :R], lo[j, t, span])

    pl.loop(0, 3)(tiles)
    for way in range(2):
        first_copy(way).wait_recv()
        first[way] += part[beside(way) * OWN + way]
        sum_copy(way).start()
    pl.loop(3, 6)(tiles)

    for way in range(2):
        plain_copy(way).wait_recv()
        out[:, spans[1 - way]] += last[way, 1 - way]
    for way in range(2):
        sum_copy(way).wait_recv()
        out[:, spans[way]] += last[way, way]
    for way in range(2):
        first_copy(way).wait_send()
        plain_copy(way).wait_send()
        sum_copy(way).wait_send()


def fold(logs, part, values, interp, cloud, points):
    vmem = pl.BlockSpec(memory_space=pltpu.VMEM)
    smem = pl.BlockSpec(memory_space=pltpu.SMEM)
    anym = pl.BlockSpec(memory_space=pl.ANY)
    dma = pltpu.SemaphoreType.DMA
    return pl.pallas_call(
        fold_kernel,
        out_shape=jax.ShapeDtypeStruct((R, COLS), F32),
        in_specs=[smem, vmem, vmem, anym, anym, anym],
        out_specs=vmem,
        scratch_shapes=[
            pltpu.VMEM((2, R, LEAF), F32),
            pltpu.VMEM((2, OWN, R, LEAF), F32),
            pltpu.VMEM((OWN, LEAF, SK), F32),
            pltpu.VMEM((6, PARTS, F, COLS), F32),
            pltpu.VMEM((F, COLS), F32),
            pltpu.VMEM((OWN, 2 * R, LEAF), BF),
            pltpu.VMEM((OWN, 4 * F, LEAF), BF),
            pltpu.VMEM((OWN, 8, LEAF), F32),
            pltpu.VMEM((OWN, LEAF, 4 * F), BF),
            pltpu.VMEM((OWN, LEAF, 128), F32),
            pltpu.VMEM((OWN, OWN, LEAF, LEAF), BF),
            pltpu.VMEM((OWN, OWN, LEAF, LEAF), BF),
            dma((8,)),
            dma((2,)), dma((2,)), dma((2, 2)), dma((2, 2)),
        ],
        compiler_params=pltpu.CompilerParams(
            collective_id=1, has_side_effects=True, vmem_limit_bytes=44 << 20
        ),
        name="fold",
    )(logs, part, values, interp, cloud, points)


def shards(
    points, weights, interp, transfer, near_count, near_src, skel_group, skel_node, far_nodes
):
    g = lax.axis_index("leaf")
    x = lax.axis_index("help") // 2
    listed = jnp.where(lax.iota(jnp.int32, NEAR)[None, :] < near_count[0][:, None], near_src, -1)
    cloud, tgt, metas, values = spread(
        points, weights, interp, transfer, skel_group, skel_node, far_nodes.T, listed
    )
    slots = metas.reshape(TGT, 1, NEAR)
    step = lax.iota(jnp.int32, SRC)
    ids = (g - 1 + step // 4) * 16 + x * 4 + step % 4
    ids = jnp.where(ids < 0, -2, ids)
    times = jnp.sum((slots == ids[None, :, None]).astype(jnp.int32), axis=2)
    logs = jnp.log2(jnp.maximum(times, 1).astype(F32))
    own_logs = jnp.where(times > 0, logs, -1e30)
    own_logs = lax.dynamic_slice_in_dim(own_logs, x * OWN, OWN, 0).reshape(-1)
    away = lax.iota(jnp.int32, TGT)[:, None] // OWN != x
    part = near(jnp.where(away, times, 0).reshape(-1), logs.reshape(-1), cloud, tgt)
    return fold(own_logs, part, values, interp, cloud, points)


def solution(mesh):
    placed = (
        P(None, ("leaf", "help")),
        P(None, ("leaf", "help")),
        P(("leaf", "help"), None, None),
        P(),
        P("leaf", "help"),
        P(("leaf", "help"), None),
        P("leaf", None),
        P(),
        P(),
    )
    return jax.shard_map(
        shards, mesh=mesh, in_specs=placed, out_specs=P(None, ("leaf", "help")), check_vma=False
    )
```
